512 devices in a mesh: layer: 128 (over z, y, x_lo), rhs: 4 (over x_hi, core).
Axes of the slice: x: 4 (x_hi: 2, x_lo: 2; x = x_hi * 2 + x_lo), y: 8, z: 8, core: 2. Of those that a mesh axis runs over, the one named last changes fastest.
Arguments:
- coupling: float32 [128, 640, 640], P('layer', 'rhs'), may hold values from -8 to 12, as said below
- density: int32 [128, 640], P('layer'), may hold values 0 or 1
- support: float32 [128, 640], P('layer'), may hold values from 0.2 to 2
- loads: float32 [128, 640, 1024], P('layer', None, 'rhs'), may hold values from -6 to 6
Outputs:
- reduced_diag: float32 [128, 640, 640], P('layer', 'rhs')
- reduced_lower: float32 [128, 640, 640], P('layer', 'rhs')
- reduced_upper: float32 [128, 640, 640], P('layer', 'rhs')
- reduced_loads: float32 [128, 640, 1024], P('layer', None, 'rhs')
The draws below stay inside these ranges and needn't reach their ends.
Inputs may be any that keep to these rules, and one draw needn't show every extreme that they name: Each coupling block is symmetric and positive definite.
All inputs are finite; a program needn't handle non-finite values. No bound on the sum of `density` on one device may be relied on, other than what follows from the above.
Results may differ from the reference program's by a relative error of at most 0.0003.
Values sent between devices are 32-bit elements; how exact they have to be, the bound alone decides.
No kernel may reach another device: no remote copies, remote signals or barrier semaphores. Data moves between devices by JAX's collectives and lax.ppermute only.
A program may use at most 64 MiB of HBM per device.

```python
import math
import jax
import jax.numpy as jnp
from jax import lax

M = 640
LEVELS = 2
LAYERS = 128
NRHS = 1024


def signed_gains(magnitude_key, sign_key, lo, hi):
    magnitude = jnp.exp(jax.random.uniform(magnitude_key, (LAYERS, M), jnp.float32, math.log(lo), math.log(hi)))
    signs = jnp.where(jax.random.bernoulli(sign_key, 0.5, (LAYERS, M)), jnp.float32(1.0), jnp.float32(-1.0))
    return magnitude * signs


def kernel_part(positions, gains, length):
    gap = jnp.abs(positions[:, :, None] - positions[:, None, :])
    return jnp.exp(-gap / length) * gains[:, :, None] * gains[:, None, :]


def draw_coupling(key, part):
    key = jax.random.fold_in(key, 11)
    keys = jax.random.split(key, 7)
    near_pos = jax.random.uniform(keys[0], (LAYERS, M), jnp.float32, 0.0, 1.0) * M
    far_pos = jax.random.uniform(keys[1], (LAYERS, M), jnp.float32, 0.0, 1.0) * M
    near_gain = signed_gains(keys[2], keys[3], 0.6, 1.6)
    far_gain = signed_gains(keys[4], keys[5], 0.6, 1.6)
    shift = jax.random.uniform(keys[6], (LAYERS, M), jnp.float32, 0.5, 1.5)
    identity = jnp.eye(M, dtype=jnp.float32)
    matrix = kernel_part(near_pos, near_gain, 4.0) + 0.5 * kernel_part(far_pos, far_gain, 16.0)
    matrix = matrix + shift[:, :, None] * identity
    return matrix


def plant(result, rng, low, top_value):
    place = [jax.random.randint(jax.random.fold_in(rng, axis), (), 0, length) for axis, length in enumerate(result.shape)]
    longest = result.shape.index(max(result.shape))
    beside = place[:longest] + [(place[longest] + 1) % result.shape[longest]] + place[longest + 1:]
    return result.at[tuple(place)].set(low).at[tuple(beside)].set(top_value)


def levels(rng, shape, shards, low, high):
    gain = 1.0
    for axis_at, shards_of in shards:
        steps = jax.random.uniform(jax.random.fold_in(jax.random.fold_in(rng, 6), axis_at), (shards_of,), jnp.float32, low / len(shards), high / len(shards))
        gain = gain * jnp.repeat(jnp.exp(steps), shape[axis_at] // shards_of).reshape((-1,) + (1,) * (len(shape) - 1 - axis_at))
    return gain


def scatter_about(own_key, extent, scale, bound, pieces=(), kind=jnp.bfloat16):
    values = jax.random.normal(own_key, extent, jnp.float32) * scale
    if len(pieces) > 0:
        values = levels(own_key, extent, pieces, -0.22, 0.18) * values
    return jnp.clip(values, min=-bound, max=bound).astype(kind)


def setup_inputs(seed: int = 0) -> dict:
    arg_keys = jax.random.split(jax.random.key(seed), 5)
    coupling = draw_coupling(jax.random.fold_in(arg_keys[4], 71), 0)
    density = plant((jax.random.randint(arg_keys[1], (LAYERS, M), 0, 4) < 3).astype(jnp.int32), jax.random.fold_in(arg_keys[1], 1), 0, 1)
    support = jnp.clip(jnp.exp(math.log(2.0) - 2.3025851 * jax.random.uniform(arg_keys[2], (LAYERS, M), jnp.float32) ** levels(arg_keys[2], (LAYERS, M), ((0, 128),), -0.2, 0.2)), 0.2, 2.0)
    loads = scatter_about(arg_keys[3], (LAYERS, M, NRHS), 1.0, 6.0, ((0, 128), (2, 4)), jnp.float32)
    return {"coupling": coupling, "density": density, "support": support, "loads": loads}


def solve_spd(factor, right):
    half = lax.linalg.triangular_solve(factor, right, left_side=True, lower=True)
    return lax.linalg.triangular_solve(factor, half, left_side=True, lower=True, transpose_a=True)

def batched(left, right):
    return jnp.einsum('lij,ljk->lik', left, right, precision=lax.Precision.HIGHEST)

def reference(coupling, density, support, loads):
    width = coupling.shape[1]
    rho = 0.3 + 0.7 * density.astype(jnp.float32)
    stiff = rho[:, :, None] * coupling * rho[:, None, :]
    zero_block = jnp.zeros_like(stiff[:1])
    below = jnp.concatenate([zero_block, stiff[:-1]], axis=0)
    identity = jnp.eye(width, dtype=jnp.float32)
    diag_block = below + stiff + support[:, :, None] * identity
    lower = -below
    upper = jnp.concatenate([-stiff[:-1], zero_block], axis=0)
    right = loads
    for level in range(LEVELS):
        dist = 2 ** level
        factor = jnp.linalg.cholesky(diag_block)
        solved_lower = solve_spd(factor, lower)
        solved_upper = solve_spd(factor, upper)
        solved_right = solve_spd(factor, right)

        def down(field):
            return jnp.concatenate([jnp.zeros_like(field[:dist]), field[:-dist]], axis=0)

        def rise(field):
            return jnp.concatenate([field[dist:], jnp.zeros_like(field[:dist])], axis=0)
        new_lower = -batched(lower, down(solved_lower))
        new_upper = -batched(upper, rise(solved_upper))
        diag_block = diag_block - batched(lower, down(solved_upper)) - batched(upper, rise(solved_lower))
        right = right - batched(lower, down(solved_right)) - batched(upper, rise(solved_right))
        lower, upper = (new_lower, new_upper)
    return (jnp.swapaxes(diag_block, 1, 2), jnp.swapaxes(lower, 1, 2), jnp.swapaxes(upper, 1, 2), right)
```

```python
import jax
import jax.numpy as jnp
from jax import lax
from jax.experimental import pallas as pl
from jax.experimental.pallas import tpu as pltpu
from jax.sharding import PartitionSpec as P

TILE = 128
ROWS = 8
AXES = ("layer", "rhs")
VMEM_BYTES = 48 * 1024 * 1024


def split3(x):
    high = x.astype(jnp.bfloat16)
    rest = x - high.astype(jnp.float32)
    mid = rest.astype(jnp.bfloat16)
    low = (rest - mid.astype(jnp.float32)).astype(jnp.bfloat16)
    return high, mid, low


def bdot(a, b):
    return jnp.dot(a, b, preferred_element_type=jnp.float32)


def thin_matmul(a, b):
    ah, am, al = split3(a)
    bh, bm, bl = split3(b)
    small = bdot(jnp.concatenate([ah, al], 1), jnp.concatenate([bl, bh], 0))
    mid = bdot(jnp.concatenate([ah, am], 1), jnp.concatenate([bm, bm], 0))
    top = bdot(jnp.concatenate([ah, am], 1), jnp.concatenate([bh, bh], 0))
    return top + (mid + small)


def exact_matmul(a, b):
    return jnp.dot(a, b, precision=lax.Precision.HIGHEST, preferred_element_type=jnp.float32)


def lanes(x, j):
    return jnp.broadcast_to(x[:, j : j + 1], (ROWS, TILE))


def subs(x, j):
    return jnp.broadcast_to(x[j : j + 1, :], (ROWS, TILE))


def invert_tile(block):
    count = TILE // ROWS
    rows = [block[ROWS * i : ROWS * i + ROWS, :] for i in range(count)]
    lane = lax.broadcasted_iota(jnp.int32, (ROWS, TILE), 1)
    sub = lax.broadcasted_iota(jnp.int32, (ROWS, TILE), 0)
    units = [jnp.where(sub == t, jnp.float32(1.0), jnp.float32(0.0)) for t in range(ROWS)]
    for p in range(count):
        k = ROWS * p
        inside = (lane >= k) & (lane < k + ROWS)
        r = rows[p]
        b = [lanes(r, k + j) for j in range(ROWS)]
        r = jnp.where(inside, jnp.where(lane - k == sub, jnp.float32(1.0), jnp.float32(0.0)), r)
        for t in range(ROWS):
            f = (b[t] - units[t]) * (1.0 / subs(b[t], t))
            for j in range(t + 1, ROWS):
                b[j] = b[j] - f * subs(b[j], t)
            r = r - f * subs(r, t)
        q = [subs(r, j) for j in range(ROWS)]
        for i in list(range(p + 1, count)) + list(range(p)):
            e = rows[i]
            acc = jnp.where(inside, jnp.float32(0.0), e)
            for j in range(ROWS):
                acc = acc - lanes(e, k + j) * q[j]
            rows[i] = acc
        rows[p] = r
    return jnp.concatenate(rows, 0)


def sweep(a_ref, block, row_start):
    col_start = pl.multiple_of(block * TILE, TILE)
    row_start = pl.multiple_of(row_start, 64)
    rows = pl.ds(row_start, TILE)
    cols = pl.ds(col_start, TILE)
    inverse = invert_tile(a_ref[rows, cols])
    solved = thin_matmul(inverse, a_ref[rows, :])
    column = a_ref[:, cols]
    a_ref[:, cols] = jnp.zeros_like(column)
    lane = lax.broadcasted_iota(jnp.int32, solved.shape, 1)
    inside = (lane >= col_start) & (lane < col_start + TILE)
    tiled = jnp.concatenate([inverse] * (solved.shape[1] // TILE), axis=1)
    solved = jnp.where(inside, tiled, solved)
    a_ref[...] = a_ref[...] - thin_matmul(column, solved)
    a_ref[rows, :] = solved


def first_kernel(half_ref, own_ref, out_ref):
    half = half_ref[0]
    size = own_ref.shape[0]
    out_ref[...] = own_ref[...]

    def body(step, carry):
        block = jnp.where(half == 0, step, 4 - step)
        sweep(out_ref, block, block * TILE - half * size)
        return carry

    lax.fori_loop(0, 2, body, 0)


def second_kernel(half_ref, own_ref, other_ref, out_ref):
    half = half_ref[0]
    size = own_ref.shape[0]
    own_rows = pl.ds(pl.multiple_of(half * size, 64), size)
    other_rows = pl.ds(pl.multiple_of((1 - half) * size, 64), size)
    done_cols = pl.multiple_of(half * 384, TILE)
    column = other_ref[:, pl.ds(done_cols, 256)]
    solved = own_ref[pl.ds(pl.multiple_of(half * 64, 64), 256), :]
    lane = lax.broadcasted_iota(jnp.int32, other_ref.shape, 1)
    done = (lane >= done_cols) & (lane < done_cols + 256)
    kept = jnp.where(done, jnp.float32(0.0), other_ref[...])
    out_ref[own_rows, :] = own_ref[...]
    out_ref[other_rows, :] = kept - exact_matmul(column, solved)

    def body(step, carry):
        block = jnp.where(half == 0, 2 + step, 2 - step)
        sweep(out_ref, block, block * TILE)
        return carry

    lax.fori_loop(0, 3, body, 0)


def invert_first(half, own):
    return pl.pallas_call(
        first_kernel,
        out_shape=jax.ShapeDtypeStruct(own.shape, jnp.float32),
        in_specs=[
            pl.BlockSpec(memory_space=pltpu.SMEM),
            pl.BlockSpec(memory_space=pltpu.VMEM),
        ],
        out_specs=pl.BlockSpec(memory_space=pltpu.VMEM),
        compiler_params=pltpu.CompilerParams(vmem_limit_bytes=VMEM_BYTES),
        name="invert_first",
    )(half, own)


def invert_second(half, own, other):
    width = own.shape[1]
    return pl.pallas_call(
        second_kernel,
        out_shape=jax.ShapeDtypeStruct((width, width), jnp.float32),
        in_specs=[
            pl.BlockSpec(memory_space=pltpu.SMEM),
            pl.BlockSpec(memory_space=pltpu.VMEM),
            pl.BlockSpec(memory_space=pltpu.VMEM),
        ],
        out_specs=pl.BlockSpec(memory_space=pltpu.VMEM),
        compiler_params=pltpu.CompilerParams(vmem_limit_bytes=VMEM_BYTES),
        name="invert_second",
    )(half, own, other)


def dot(a, b, dims, precision):
    return lax.dot_general(
        a, b, (dims, ((), ())), precision=precision, preferred_element_type=jnp.float32
    )


NN = ((1,), (0,))
NT = ((1,), (1,))
TN = ((0,), (0,))
FULL = lax.Precision.HIGHEST
THREE = lax.Precision.HIGH


def device(layer, half, core):
    return layer * 4 + half * 2 + core


def pairs_of(count, moves):
    pairs = []
    for layer in range(count):
        for half in range(2):
            for core, up, across, onto in moves:
                if 0 <= layer + up < count:
                    pairs.append(
                        (device(layer, half, core), device(layer + up, half ^ across, onto))
                    )
    return pairs


def shards(coupling, density, support, loads):
    part = coupling.shape[1]
    width = coupling.shape[2]
    layers = lax.axis_size("layer")
    layer = lax.axis_index("layer")
    place = lax.axis_index("rhs")
    half = place // 2
    core = place % 2
    upper = core == 1

    def move(array, *moves):
        return lax.ppermute(array, AXES, pairs_of(layers, moves))

    def straight(array, by):
        return move(array, (0, by, 0, 0), (1, -by, 0, 1))

    def crossed(array, by):
        return move(array, (1, by, 0, 0), (0, -by, 0, 1))

    def sibling(array):
        return move(array, (0, 0, 0, 1), (1, 0, 0, 0))

    def opposite(array):
        return move(array, (0, 0, 1, 0), (1, 0, 1, 1))

    def pick(on_upper, on_lower):
        return jnp.where(upper, on_upper, on_lower)

    def halves(own, other):
        return jnp.concatenate([jnp.where(half == 0, own, other), jnp.where(half == 0, other, own)], 0)

    half_arg = half.astype(jnp.int32).reshape(1)
    span = 2 * part
    row = lax.broadcasted_iota(jnp.int32, (span, width), 0)
    col = lax.broadcasted_iota(jnp.int32, (span, width), 1)
    own_diag = col == row + half * span
    other_diag = col == row + (1 - half) * span

    rho = 0.3 + 0.7 * density[0].astype(jnp.float32)
    rho_rows = lax.dynamic_slice_in_dim(rho, place * part, part, 0)
    stiff = rho_rows[:, None] * coupling[0] * rho[None, :]
    ones = jnp.ones((ROWS - 1, width), jnp.float32)
    tagged = jnp.concatenate([stiff, support, ones], axis=0)

    near_a = straight(tagged, 1)
    near_b = crossed(stiff, 1)
    far_a = move(stiff, (0, 2, 0, 0))
    far_b = move(stiff, (1, 2, 0, 0), (0, 0, 0, 1))
    side_support = near_a[part]
    side_support = jnp.where(near_a[part + 1] > 0.5, side_support, jnp.float32(1.0))
    near_a = near_a[:part]
    x_own = jnp.concatenate([pick(far_b, near_a), pick(stiff, near_b)], axis=0)
    y_own = jnp.concatenate([pick(near_b, far_a), pick(near_a, far_b)], axis=0)
    d_own = (x_own + y_own) + jnp.where(own_diag, side_support[None, :], jnp.float32(0.0))

    loads_0 = loads[0]
    d_other = opposite(d_own)
    started = invert_first(half_arg, d_own)
    x_other = opposite(x_own)
    load_a = straight(loads_0, 1)
    load_b = crossed(loads_0, 1)
    inverse = invert_second(half_arg, started, d_other)

    x_full = halves(x_own, x_other)
    y_other = (d_other - x_other) - jnp.where(
        other_diag, side_support[None, :], jnp.float32(0.0)
    )
    y_full = halves(y_own, y_other)
    live = jnp.where(upper & (layer == layers - 1), jnp.float32(0.0), jnp.float32(1.0))
    live_far = jnp.where(upper & (layer == layers - 2), jnp.float32(0.0), jnp.float32(1.0))
    g_own = live * dot(x_own, inverse, NN, FULL)
    rest_own = x_own - dot(g_own, x_full, NN, FULL)
    g_other = live * dot(x_other, inverse, NN, FULL)
    rest_other = x_other - dot(g_other, x_full, NN, FULL)
    new_own = rest_own + sibling(rest_own) + jnp.where(own_diag, support, jnp.float32(0.0))
    new_other = rest_other + sibling(rest_other) + jnp.where(other_diag, support, jnp.float32(0.0))

    g_full = halves(g_own, g_other)
    link_t = -live_far * dot(y_full, g_full, NT, THREE)
    near_loads = jnp.concatenate([pick(load_b, load_a), pick(load_a, load_b)], axis=1)
    cases = loads_0.shape[1]
    load_part = dot(g_full, near_loads, NN, THREE)
    load_sent = pick(load_part[:, :cases], load_part[:, cases:])
    load_kept = pick(load_part[:, cases:], load_part[:, :cases])
    new_loads = loads_0 + load_kept + sibling(load_sent)

    has_side = pick(layer + 2 < layers, layer >= 2)
    lone = jnp.where(has_side, jnp.float32(0.0), jnp.float32(1.0))
    d_own = straight(new_own, 2) + jnp.where(own_diag, lone, jnp.float32(0.0))
    d_other = straight(new_other, 2) + jnp.where(other_diag, lone, jnp.float32(0.0))
    started = invert_first(half_arg, d_own)
    far_link = straight(lax.dynamic_slice_in_dim(link_t, half * span, span, 0), 2)
    load_a = straight(new_loads, 2)
    load_b = crossed(new_loads, 2)
    inverse = invert_second(half_arg, started, d_other)

    solved = dot(inverse, link_t, NN, THREE)
    link_cols = lax.dynamic_slice_in_dim(link_t, half * span, span, 1)
    diag_part = dot(link_cols, solved, TN, THREE)
    link_part = -dot(far_link, solved, NN, THREE)
    near_loads = jnp.concatenate([pick(load_b, load_a), pick(load_a, load_b)], axis=1)
    load_part = dot(solved, near_loads, TN, THREE)

    def kept(array):
        return pick(array[part:], array[:part])

    def sent(array):
        return pick(array[:part], array[part:])

    diag_in = sibling(sent(diag_part))
    link_in = sibling(sent(link_part))
    load_sent = pick(load_part[:, :cases], load_part[:, cases:])
    load_kept = pick(load_part[:, cases:], load_part[:, :cases])
    diag_out = kept(new_own) - kept(diag_part) - diag_in
    mine = kept(link_part)
    lower_out = pick(link_in, mine)
    upper_out = pick(mine, link_in)
    loads_out = new_loads - load_kept - sibling(load_sent)
    return (diag_out[None], lower_out[None], upper_out[None], loads_out[None])


def solution(mesh):
    placed = (P("layer", "rhs", None), P("layer", None), P("layer", None), P("layer", None, "rhs"))
    return jax.shard_map(
        shards,
        mesh=mesh,
        in_specs=placed,
        out_specs=(
            P("layer", "rhs", None),
            P("layer", "rhs", None),
            P("layer", "rhs", None),
            P("layer", None, "rhs"),
        ),
        check_vma=False,
    )
```

```python
import functools

import jax
import jax.numpy as jnp
from jax import lax
from jax.experimental import pallas as pl
from jax.experimental.pallas import tpu as pltpu
from jax.sharding import PartitionSpec as P

TILE = 128
ROWS = 8
AXES = ("layer", "rhs")
VMEM_BYTES = 28 * 1024 * 1024


def split3(x):
    high = x.astype(jnp.bfloat16)
    rest = x - high.astype(jnp.float32)
    mid = rest.astype(jnp.bfloat16)
    low = (rest - mid.astype(jnp.float32)).astype(jnp.bfloat16)
    return high, mid, low


def bdot(a, b):
    return jnp.dot(a, b, preferred_element_type=jnp.float32)


def thin_matmul(a, b):
    ah, am, al = split3(a)
    bh, bm, bl = split3(b)
    small = bdot(jnp.concatenate([ah, al], 1), jnp.concatenate([bl, bh], 0))
    mid = bdot(jnp.concatenate([ah, am], 1), jnp.concatenate([bm, bm], 0))
    top = bdot(jnp.concatenate([ah, am], 1), jnp.concatenate([bh, bh], 0))
    return top + (mid + small)


def six_pass(a, b, across=False):
    ah, am, al = split3(a)
    bh, bm, bl = split3(b)
    left = jnp.concatenate([al, ah, am, am, ah, ah], 1)
    side = 1 if across else 0
    right = jnp.concatenate([bh, bl, bm, bh, bm, bh], side)
    return lax.dot_general(
        left, right, (((1,), (side,)), ((), ())), preferred_element_type=jnp.float32
    )


def split2(x):
    high = x.astype(jnp.bfloat16)
    return high, (x - high.astype(jnp.float32)).astype(jnp.bfloat16)


def three_pass(a, b, across=False):
    ah, al = split2(a)
    bh, bl = split2(b)
    left = jnp.concatenate([al, ah, ah], 1)
    side = 1 if across else 0
    right = jnp.concatenate([bh, bl, bh], side)
    return lax.dot_general(
        left, right, (((1,), (side,)), ((), ())), preferred_element_type=jnp.float32
    )


def lanes(x, j):
    return jnp.broadcast_to(x[:, j : j + 1], (ROWS, TILE))


def subs(x, j):
    return jnp.broadcast_to(x[j : j + 1, :], (ROWS, TILE))


def tree_sum(terms):
    terms = list(terms)
    while len(terms) > 1:
        terms = [sum(terms[i : i + 2][1:], terms[i]) for i in range(0, len(terms), 2)]
    return terms[0]


def short_matmul(a, b):
    ah, am, al = split3(a)
    bh, bm, bl = split3(b)
    return bdot(
        jnp.concatenate([al, ah, am, am, ah, ah], 1), jnp.concatenate([bh, bl, bm, bh, bm, bh], 0)
    )


GROUP = 2


def invert_tile(block):
    count = TILE // ROWS
    span = GROUP * ROWS
    rows = [block[ROWS * i : ROWS * i + ROWS, :] for i in range(count)]
    lane = lax.broadcasted_iota(jnp.int32, (ROWS, TILE), 1)
    sub = lax.broadcasted_iota(jnp.int32, (ROWS, TILE), 0)
    units = [jnp.where(sub == t, jnp.float32(1.0), jnp.float32(0.0)) for t in range(ROWS)]
    b = [lanes(rows[0], j) for j in range(ROWS)]
    for first in range(0, count, GROUP):
        now = list(range(first, first + GROUP))
        soon = [i for i in range(first + GROUP, first + 2 * GROUP) if i < count]
        rest = [i for i in range(count) if i not in now and i not in soon]
        before = list(rows)
        for p in now:
            k = ROWS * p
            inside = (lane >= k) & (lane < k + ROWS)
            r = rows[p]
            ahead = []
            if p + 1 < count:
                ahead = [lanes(r, k + ROWS + j) for j in range(ROWS)]
                below = [lanes(rows[p + 1], k + j) for j in range(ROWS)]
                beyond = [lanes(rows[p + 1], k + ROWS + j) for j in range(ROWS)]
            r = jnp.where(inside, jnp.where(lane - k == sub, jnp.float32(1.0), jnp.float32(0.0)), r)
            for t in range(0, ROWS, 2):
                top = subs(b[t], t)
                side = subs(b[t + 1], t)
                low = subs(b[t + 1], t + 1)
                inverse = 1.0 / (top * low - side * side)
                f = (b[t] - units[t]) * (1.0 / top)
                w = ((b[t + 1] - f * side) - units[t + 1]) * top
                g = w * inverse

                def eliminate(x, hurry=False):
                    x = x - f * subs(x, t)
                    other = subs(x, t + 1)
                    return x - ((w * other) * inverse if hurry else g * other)

                for j in range(t + 2, ROWS):
                    b[j] = eliminate(b[j], j < t + 4)
                r = eliminate(r)
                ahead = [eliminate(x) for x in ahead]
            if ahead:
                b = [
                    beyond[j] - tree_sum(below[m] * subs(ahead[j], m) for m in range(ROWS))
                    for j in range(ROWS)
                ]
            q = [subs(r, j) for j in range(ROWS)]
            for i in [i for i in now + soon if i > p] + [i for i in now if i < p]:
                e = rows[i]
                spread = below if i == p + 1 else [lanes(e, k + j) for j in range(ROWS)]
                kept = jnp.where(inside, jnp.float32(0.0), e)
                rows[i] = kept - tree_sum(spread[j] * q[j] for j in range(ROWS))
            rows[p] = r
        start = first * ROWS
        solved = jnp.concatenate([rows[i] for i in now], 0)
        for part in ([i for i in rest if i > first], [i for i in rest if i < first]):
            if part:
                c = jnp.concatenate([before[i] for i in part], 0)
                wide = lax.broadcasted_iota(jnp.int32, c.shape, 1)
                done = (wide >= start) & (wide < start + span)
                update = short_matmul(c[:, start : start + span], solved)
                c = jnp.where(done, jnp.float32(0.0), c) - update
                for m, i in enumerate(part):
                    rows[i] = c[ROWS * m : ROWS * m + ROWS, :]
    return jnp.concatenate(rows, 0)


def sweep(a_ref, block, row_start):
    col_start = pl.multiple_of(block * TILE, TILE)
    row_start = pl.multiple_of(row_start, 64)
    rows = pl.ds(row_start, TILE)
    cols = pl.ds(col_start, TILE)
    inverse = invert_tile(a_ref[rows, cols])
    solved = thin_matmul(inverse, a_ref[rows, :])
    column = a_ref[:, cols]
    a_ref[:, cols] = jnp.zeros_like(column)
    lane = lax.broadcasted_iota(jnp.int32, solved.shape, 1)
    inside = (lane >= col_start) & (lane < col_start + TILE)
    tiled = jnp.concatenate([inverse] * (solved.shape[1] // TILE), axis=1)
    solved = jnp.where(inside, tiled, solved)
    a_ref[...] = a_ref[...] - thin_matmul(column, solved)
    a_ref[rows, :] = solved


SMEM = pl.BlockSpec(memory_space=pltpu.SMEM)
VMEM = pl.BlockSpec(memory_space=pltpu.VMEM)
HALF, CORE, LIVE, LIVE_FAR, LONE = range(5)


def local_call(body, name, micros, flags, inputs, shapes, scratch=()):
    out = pl.pallas_call(
        body,
        out_shape=[jax.ShapeDtypeStruct(shape, jnp.float32) for shape in shapes],
        in_specs=[SMEM] + [VMEM] * len(inputs),
        out_specs=[VMEM] * len(shapes),
        scratch_shapes=[pltpu.VMEM(shape, jnp.float32) for shape in scratch],
        compiler_params=pltpu.CompilerParams(vmem_limit_bytes=VMEM_BYTES),
        cost_estimate=pl.CostEstimate(
            flops=int(micros * 1.1e9), transcendentals=0, bytes_accessed=int(micros * 3.5e6)
        ),
        name=name,
    )(flags, *inputs)
    return out


def rows_of(half, size):
    return pl.ds(pl.multiple_of(half * size, 64), size)


def lone_diag(flags, offset, shape):
    row = lax.broadcasted_iota(jnp.int32, shape, 0) + offset
    col = lax.broadcasted_iota(jnp.int32, shape, 1)
    lone = jnp.where(flags[LONE] == 1, jnp.float32(1.0), jnp.float32(0.0))
    return jnp.where(row == col, lone, jnp.float32(0.0))


def factor_of(flag):
    return jnp.where(flag == 1, jnp.float32(1.0), jnp.float32(0.0))


def first_kernel(flags, own_ref, out_ref):
    half = flags[HALF]
    size = own_ref.shape[0]
    out_ref[...] = own_ref[...] + lone_diag(flags, half * size, own_ref.shape)

    def body(step, carry):
        block = jnp.where(half == 0, step, 4 - step)
        sweep(out_ref, block, block * TILE - half * size)
        return carry

    lax.fori_loop(0, 2, body, 0)


def complete(half, own_ref, square, turned_ref, full_ref):
    size = own_ref.shape[0]
    own = own_ref[...]
    turned_ref[...] = own.T
    full_ref[rows_of(half, size), :] = own

    @pl.when(half == 0)
    def _():
        full_ref[size:, :size] = turned_ref[size:, :]
        full_ref[size:, size:] = square

    @pl.when(half == 1)
    def _():
        full_ref[:size, size:] = turned_ref[:size, :]
        full_ref[:size, :size] = square


def second_kernel(first_col, flags, own_ref, swept_ref, square_ref, out_ref, turned_ref):
    half = flags[HALF]
    size = own_ref.shape[0]
    square = square_ref[:, first_col : first_col + size]
    complete(half, own_ref, square, turned_ref, out_ref)
    other_rows = rows_of(1 - half, size)
    done_cols = pl.multiple_of(half * 384, TILE)
    column = out_ref[other_rows, pl.ds(done_cols, 256)]
    solved = swept_ref[pl.ds(pl.multiple_of(half * 64, 64), 256), :]
    shape = own_ref.shape
    lane = lax.broadcasted_iota(jnp.int32, shape, 1)
    done = (lane >= done_cols) & (lane < done_cols + 256)
    other = out_ref[other_rows, :] + lone_diag(flags, (1 - half) * size, shape)
    out_ref[rows_of(half, size), :] = swept_ref[...]
    out_ref[other_rows, :] = jnp.where(done, jnp.float32(0.0), other) - six_pass(column, solved)

    def body(step, carry):
        block = jnp.where(half == 0, 2 + step, 2 - step)
        sweep(out_ref, block, block * TILE)
        return carry

    lax.fori_loop(0, 3, body, 0)


def rest_kernel(flags, inverse_ref, x_ref, square_ref, g_ref, rest_ref, turned_ref, full_ref):
    half = flags[HALF]
    size, width = x_ref.shape
    complete(half, x_ref, square_ref[...], turned_ref, full_ref)
    g_ref[...] = factor_of(flags[LIVE]) * six_pass(full_ref[...], inverse_ref[...])
    own_rows, other_rows = rows_of(half, size), rows_of(1 - half, size)
    rest_ref[:, :width] = x_ref[...] - six_pass(g_ref[own_rows, :], full_ref[...])
    rest_ref[:, width : width + size] = square_ref[...] - six_pass(
        g_ref[other_rows, :], full_ref[other_rows, :], across=True
    )
    rest_ref[:, width + size :] = jnp.zeros_like(rest_ref[:, width + size :])


def link_kernel(flags, g_ref, y_ref, y_square_ref, link_ref, turned_link_ref, turned_ref, full_ref):
    complete(flags[HALF], y_ref, y_square_ref[...], turned_ref, full_ref)
    live = -factor_of(flags[LIVE_FAR])
    g = g_ref[...]
    link_ref[...] = live * three_pass(g, full_ref[...])
    turned_link_ref[...] = live * three_pass(y_ref[...], g, across=True)


def combine_kernel(flags, rest_ref, came_ref, diag_ref, link_ref, own_out, packed_out):
    size, width = own_out.shape
    row = lax.broadcasted_iota(jnp.int32, (size, width), 0) + flags[HALF] * size
    col = lax.broadcasted_iota(jnp.int32, (size, width), 1)
    own_diag = jnp.where(row == col, diag_ref[:, :width], jnp.float32(0.0))
    own_out[...] = rest_ref[:, :width] + came_ref[:, :width] + own_diag
    tail = rest_ref.shape[1] - width
    row = lax.broadcasted_iota(jnp.int32, (size, tail), 0)
    col = lax.broadcasted_iota(jnp.int32, (size, tail), 1)
    square_diag = jnp.where(row == col, diag_ref[:, width:], jnp.float32(0.0))
    packed_out[:, :width] = link_ref[...]
    packed_out[:, width:] = rest_ref[:, width:] + came_ref[:, width:] + square_diag


def near_kernel(flags, g_ref, loads_ref, part_ref):
    part_ref[...] = three_pass(g_ref[...], loads_ref[...])


def post_kernel(flags, inverse_ref, link_ref, far_ref, diag_ref, g_ref, kept_ref, sent_ref, part_ref):
    half, core = flags[HALF], flags[CORE]
    size, width = diag_ref.shape
    link = link_ref[...]
    both = three_pass(jnp.concatenate([link, far_ref[:, :width]], 0), inverse_ref[...])
    g_ref[...] = both[:width]
    left = jnp.concatenate([g_ref[rows_of(half, size), :], both[width:]], 0)
    part_ref[...] = three_pass(left, link, across=True)
    part = size // 2
    keep = pl.multiple_of(core * part, 32)
    send = pl.multiple_of((1 - core) * part, 32)
    kept_ref[:part, :] = diag_ref[pl.ds(keep, part), :] - part_ref[pl.ds(keep, part), :]
    kept_ref[part:, :] = -part_ref[pl.ds(size + keep, part), :]
    sent_ref[:part, :] = -part_ref[pl.ds(send, part), :]
    sent_ref[part:, :] = -part_ref[pl.ds(size + send, part), :]


def last_kernel(flags, g_ref, loads_ref, near_ref, kept_ref, sent_ref, part_ref):
    core = flags[CORE]
    width = kept_ref.shape[1]
    part_ref[...] = three_pass(g_ref[...], near_ref[...])
    keep = pl.ds(pl.multiple_of(core * width, width), width)
    send = pl.ds(pl.multiple_of((1 - core) * width, width), width)
    kept_ref[...] = loads_ref[:, keep] - part_ref[:, keep]
    sent_ref[...] = -part_ref[:, send]


def device(layer, half, core):
    return layer * 4 + half * 2 + core


def pairs_of(count, moves):
    pairs = []
    for layer in range(count):
        for half in range(2):
            for core, up, across, onto in moves:
                if 0 <= layer + up < count:
                    pairs.append(
                        (device(layer, half, core), device(layer + up, half ^ across, onto))
                    )
    return pairs


def after(array, *others):
    return lax.optimization_barrier((array,) + others)[0]


def shards(coupling, density, support, loads):
    part = coupling.shape[1]
    width = coupling.shape[2]
    layers = lax.axis_size("layer")
    layer = lax.axis_index("layer")
    place = lax.axis_index("rhs")
    half = place // 2
    core = place % 2
    upper = core == 1

    def move(array, *moves):
        return lax.ppermute(array, AXES, pairs_of(layers, moves))

    def straight(array, by):
        return move(array, (0, by, 0, 0), (1, -by, 0, 1))

    def crossed(array, by):
        return move(array, (1, by, 0, 0), (0, -by, 0, 1))

    def sibling(array):
        return move(array, (0, 0, 0, 1), (1, 0, 0, 0))

    def opposite(array):
        return move(array, (0, 0, 1, 0), (1, 0, 1, 1))

    def pick(on_upper, on_lower):
        return jnp.where(upper, on_upper, on_lower)

    span = 2 * part
    cases = loads.shape[2]

    def square(array, first):
        return jnp.where(first == 0, array[:, :span], array[:, span:])

    live = jnp.logical_not(upper & (layer == layers - 1))
    live_far = jnp.logical_not(upper & (layer == layers - 2))
    lone = jnp.logical_not(pick(layer + 2 < layers, layer >= 2))
    zero = jnp.zeros((), jnp.int32)
    flags_0 = jnp.stack([half, core, live, live_far, zero]).astype(jnp.int32)
    flags_1 = jnp.stack([half, core, live, live_far, lone]).astype(jnp.int32)
    row = lax.broadcasted_iota(jnp.int32, (span, width), 0)
    col = lax.broadcasted_iota(jnp.int32, (span, width), 1)
    own_diag = col == row + half * span
    square_diag = row[:, :span] == col[:, :span]

    rho = 0.3 + 0.7 * density[0].astype(jnp.float32)
    rho_rows = lax.dynamic_slice_in_dim(rho, place * part, part, 0)
    stiff = rho_rows[:, None] * coupling[0] * rho[None, :]
    ones = jnp.ones((ROWS - 1, width), jnp.float32)
    tagged = jnp.concatenate([stiff, support, ones], axis=0)

    near_a = straight(tagged, 1)
    near_b = crossed(stiff, 1)
    far_a = move(stiff, (0, 2, 0, 0))
    far_b = move(stiff, (1, 2, 0, 0), (0, 0, 0, 1))
    side_support = jnp.where(near_a[part + 1] > 0.5, near_a[part], jnp.float32(1.0))
    near_a = near_a[:part]
    x_own = jnp.concatenate([pick(far_b, near_a), pick(stiff, near_b)], axis=0)
    y_own = jnp.concatenate([pick(near_b, far_a), pick(near_a, far_b)], axis=0)
    d_own = (x_own + y_own) + jnp.where(own_diag, side_support[None, :], jnp.float32(0.0))

    d_square = opposite(square(d_own, half))
    own_shape = (span, width)
    full_shape = (width, width)
    packed_shape = (span, width + 3 * TILE)
    load_shape = (width, cases)
    pair_shape = (width, 2 * cases)
    turned_shape = (width, span)

    loads_0 = loads[0]
    loads_in = sibling(loads_0)
    loads_0 = jnp.concatenate([pick(loads_in, loads_0), pick(loads_0, loads_in)], axis=1)
    (swept_0,) = local_call(first_kernel, "invert_first", 9, flags_0, [d_own], [own_shape])
    x_square = opposite(after(square(x_own, half), swept_0))
    near_loads = straight(after(loads_0, swept_0), 1)
    (inverse,) = local_call(
        functools.partial(second_kernel, 0), "invert_second", 14, flags_0,
        [d_own, swept_0, d_square], [full_shape], [turned_shape],
    )
    g_full, rest = local_call(
        rest_kernel, "rest", 1, flags_0, [inverse, x_own, x_square],
        [full_shape, packed_shape], [turned_shape, full_shape],
    )
    rest_in = sibling(rest)
    other_side = jnp.where(half == 0, side_support[span:], side_support[:span])
    y_square = (d_square - x_square) - jnp.where(square_diag, other_side[None, :], jnp.float32(0.0))
    link, turned_link = local_call(
        link_kernel, "links", 5, flags_0, [g_full, after(y_own, near_loads), y_square],
        [full_shape, own_shape], [turned_shape, full_shape],
    )
    other_support = jnp.where(half == 0, support[:, span:], support[:, :span])
    rest_diag = jnp.concatenate([support, other_support, jnp.zeros((1, 3 * TILE - span))], axis=1)
    new_own, packed = local_call(
        combine_kernel, "combine", 1, flags_0, [rest, rest_in, rest_diag, turned_link],
        [own_shape, packed_shape],
    )
    d_own = straight(new_own, 2)
    packed = straight(packed, 2)
    (near_part,) = local_call(
        near_kernel, "near_loads", 2, flags_0, [after(g_full, new_own), near_loads], [pair_shape]
    )
    new_loads = loads_0 + near_part + sibling(near_part)

    (swept,) = local_call(first_kernel, "invert_first", 9, flags_1, [d_own], [own_shape])
    near_loads = straight(after(new_loads, swept), 2)
    (inverse,) = local_call(
        functools.partial(second_kernel, width), "invert_second", 14, flags_1,
        [d_own, swept, packed], [full_shape], [turned_shape],
    )
    g_full, kept, sent = local_call(
        post_kernel, "last_blocks", 6, flags_1, [inverse, link, packed, new_own],
        [full_shape, own_shape, own_shape], [full_shape],
    )
    came = sibling(sent)
    load_kept, load_sent = local_call(
        last_kernel, "last_loads", 2, flags_1, [g_full, new_loads, near_loads],
        [load_shape, load_shape], [pair_shape],
    )
    loads_out = load_kept + sibling(load_sent)
    diag_out = kept[:part] + came[:part]
    lower_out = pick(came[part:], kept[part:])
    upper_out = pick(kept[part:], came[part:])
    return (diag_out[None], lower_out[None], upper_out[None], loads_out[None])


def solution(mesh):
    placed = (P("layer", "rhs", None), P("layer", None), P("layer", None), P("layer", None, "rhs"))
    return jax.shard_map(
        shards,
        mesh=mesh,
        in_specs=placed,
        out_specs=(
            P("layer", "rhs", None),
            P("layer", "rhs", None),
            P("layer", "rhs", None),
            P("layer", None, "rhs"),
        ),
        check_vma=False,
    )
```

```python
import functools

import jax
import jax.numpy as jnp
from jax import lax
from jax.experimental import pallas as pl
from jax.experimental.pallas import tpu as pltpu
from jax.sharding import PartitionSpec as P

TILE = 128
ROWS = 8
AXES = ("layer", "rhs")


def split3(x):
    high = x.astype(jnp.bfloat16)
    rest = x - high.astype(jnp.float32)
    mid = rest.astype(jnp.bfloat16)
    low = (rest - mid.astype(jnp.float32)).astype(jnp.bfloat16)
    return high, mid, low


def bdot(a, b):
    return jnp.dot(a, b, preferred_element_type=jnp.float32)


def thin_matmul(a, b):
    ah, am, al = split3(a)
    bh, bm, bl = split3(b)
    small = bdot(jnp.concatenate([ah, al], 1), jnp.concatenate([bl, bh], 0))
    mid = bdot(jnp.concatenate([ah, am], 1), jnp.concatenate([bm, bm], 0))
    top = bdot(jnp.concatenate([ah, am], 1), jnp.concatenate([bh, bh], 0))
    return top + (mid + small)


def product(a, b, across):
    dims = (((1,), (1 if across else 0,)), ((), ()))
    return lax.dot_general(a, b, dims, preferred_element_type=jnp.float32)


def six_pass(a, b, across=False):
    ah, am, al = split3(a)
    bh, bm, bl = split3(b)
    small = product(am, bm, across) + product(ah, bl, across) + product(al, bh, across)
    return product(ah, bh, across) + (product(ah, bm, across) + product(am, bh, across) + small)


def split2(x):
    high = x.astype(jnp.bfloat16)
    return high, (x - high.astype(jnp.float32)).astype(jnp.bfloat16)


def three_pass(a, b, across=False):
    ah, al = split2(a)
    bh, bl = split2(b)
    return product(ah, bh, across) + (product(ah, bl, across) + product(al, bh, across))


def lanes(x, j):
    return jnp.broadcast_to(x[:, j : j + 1], (ROWS, TILE))


def subs(x, j):
    return jnp.broadcast_to(x[j : j + 1, :], (ROWS, TILE))


def tree_sum(terms):
    terms = list(terms)
    while len(terms) > 1:
        terms = [sum(terms[i : i + 2][1:], terms[i]) for i in range(0, len(terms), 2)]
    return terms[0]


def short_matmul(a, b):
    ah, am, al = split3(a)
    bh, bm, bl = split3(b)
    return bdot(
        jnp.concatenate([al, ah, am, am, ah, ah], 1), jnp.concatenate([bh, bl, bm, bh, bm, bh], 0)
    )


GROUP = 2


def invert_tile(block):
    count = TILE // ROWS
    span = GROUP * ROWS
    rows = [block[ROWS * i : ROWS * i + ROWS, :] for i in range(count)]
    lane = lax.broadcasted_iota(jnp.int32, (ROWS, TILE), 1)
    sub = lax.broadcasted_iota(jnp.int32, (ROWS, TILE), 0)
    units = [jnp.where(sub == t, jnp.float32(1.0), jnp.float32(0.0)) for t in range(ROWS)]
    b = [lanes(rows[0], j) for j in range(ROWS)]
    for first in range(0, count, GROUP):
        now = list(range(first, first + GROUP))
        soon = [i for i in range(first + GROUP, first + 2 * GROUP) if i < count]
        rest = [i for i in range(count) if i not in now and i not in soon]
        before = list(rows)
        for p in now:
            k = ROWS * p
            inside = (lane >= k) & (lane < k + ROWS)
            r = rows[p]
            ahead = []
            if p + 1 < count:
                ahead = [lanes(r, k + ROWS + j) for j in range(ROWS)]
                below = [lanes(rows[p + 1], k + j) for j in range(ROWS)]
                beyond = [lanes(rows[p + 1], k + ROWS + j) for j in range(ROWS)]
            r = jnp.where(inside, jnp.where(lane - k == sub, jnp.float32(1.0), jnp.float32(0.0)), r)
            for t in range(0, ROWS, 2):
                top = subs(b[t], t)
                side = subs(b[t + 1], t)
                low = subs(b[t + 1], t + 1)
                inverse = 1.0 / (top * low - side * side)
                f = (b[t] - units[t]) * (1.0 / top)
                w = ((b[t + 1] - f * side) - units[t + 1]) * top
                g = w * inverse

                def eliminate(x, hurry=False):
                    x = x - f * subs(x, t)
                    other = subs(x, t + 1)
                    return x - ((w * other) * inverse if hurry else g * other)

                for j in range(t + 2, ROWS):
                    b[j] = eliminate(b[j], j < t + 4)
                r = eliminate(r)
                ahead = [eliminate(x) for x in ahead]
            if ahead:
                b = [
                    beyond[j] - tree_sum(below[m] * subs(ahead[j], m) for m in range(ROWS))
                    for j in range(ROWS)
                ]
            q = [subs(r, j) for j in range(ROWS)]
            for i in [i for i in now + soon if i > p] + [i for i in now if i < p]:
                e = rows[i]
                spread = below if i == p + 1 else [lanes(e, k + j) for j in range(ROWS)]
                kept = jnp.where(inside, jnp.float32(0.0), e)
                rows[i] = kept - tree_sum(spread[j] * q[j] for j in range(ROWS))
            rows[p] = r
        start = first * ROWS
        solved = jnp.concatenate([rows[i] for i in now], 0)
        for part in ([i for i in rest if i > first], [i for i in rest if i < first]):
            if part:
                c = jnp.concatenate([before[i] for i in part], 0)
                wide = lax.broadcasted_iota(jnp.int32, c.shape, 1)
                done = (wide >= start) & (wide < start + span)
                update = short_matmul(c[:, start : start + span], solved)
                c = jnp.where(done, jnp.float32(0.0), c) - update
                for m, i in enumerate(part):
                    rows[i] = c[ROWS * m : ROWS * m + ROWS, :]
    return jnp.concatenate(rows, 0)


def sweep(a_ref, block, row_start):
    col_start = pl.multiple_of(block * TILE, TILE)
    row_start = pl.multiple_of(row_start, 64)
    rows = pl.ds(row_start, TILE)
    cols = pl.ds(col_start, TILE)
    inverse = invert_tile(a_ref[rows, cols])
    solved = thin_matmul(inverse, a_ref[rows, :])
    column = a_ref[:, cols]
    a_ref[:, cols] = jnp.zeros_like(column)
    lane = lax.broadcasted_iota(jnp.int32, solved.shape, 1)
    inside = (lane >= col_start) & (lane < col_start + TILE)
    tiled = jnp.concatenate([inverse] * (solved.shape[1] // TILE), axis=1)
    solved = jnp.where(inside, tiled, solved)
    a_ref[...] = a_ref[...] - thin_matmul(column, solved)
    a_ref[rows, :] = solved


SMEM = pl.BlockSpec(memory_space=pltpu.SMEM)
VMEM = pl.BlockSpec(memory_space=pltpu.VMEM)
HALF, CORE, LIVE, LIVE_FAR, LONE = range(5)


def local_call(body, name, micros, mebibytes, flags, inputs, shapes, scratch=()):
    out = pl.pallas_call(
        body,
        out_shape=[jax.ShapeDtypeStruct(shape, jnp.float32) for shape in shapes],
        in_specs=[SMEM] + [VMEM] * len(inputs),
        out_specs=[VMEM] * len(shapes),
        scratch_shapes=[pltpu.VMEM(shape, jnp.float32) for shape in scratch],
        compiler_params=pltpu.CompilerParams(vmem_limit_bytes=mebibytes * 1024 * 1024),
        cost_estimate=pl.CostEstimate(
            flops=int(micros * 1.1e9), transcendentals=0, bytes_accessed=int(micros * 3.5e6)
        ),
        name=name,
    )(flags, *inputs)
    return out


def rows_of(half, size):
    return pl.ds(pl.multiple_of(half * size, 64), size)


def lone_diag(flags, offset, shape):
    row = lax.broadcasted_iota(jnp.int32, shape, 0) + offset
    col = lax.broadcasted_iota(jnp.int32, shape, 1)
    lone = jnp.where(flags[LONE] == 1, jnp.float32(1.0), jnp.float32(0.0))
    return jnp.where(row == col, lone, jnp.float32(0.0))


def factor_of(flag):
    return jnp.where(flag == 1, jnp.float32(1.0), jnp.float32(0.0))


def gather_kernel(
    flags, own_ref, far_a_ref, far_b_ref, near_a_ref, near_b_ref,
    x_ref, y_ref, d_ref, d_square_ref, x_square_ref, side_ref,
):
    half = flags[HALF]
    upper = flags[CORE] == 1
    size, width = x_ref.shape
    part = size // 2
    near_a, near_b = near_a_ref[:part, :], near_b_ref[:part, :]
    far_a, far_b = far_a_ref[:part, :], far_b_ref[:part, :]
    x_ref[:part, :] = jnp.where(upper, far_b, near_a)
    x_ref[part:, :] = jnp.where(upper, own_ref[:part, :], near_b)
    y_ref[:part, :] = jnp.where(upper, near_b, far_a)
    y_ref[part:, :] = jnp.where(upper, near_a, far_b)
    side = jnp.where(
        near_a_ref[part + 1 : part + 2, :] > 0.5, near_a_ref[part : part + 1, :], jnp.float32(1.0)
    )
    row = lax.broadcasted_iota(jnp.int32, (size, width), 0) + half * size
    col = lax.broadcasted_iota(jnp.int32, (size, width), 1)
    d_ref[...] = (x_ref[...] + y_ref[...]) + jnp.where(row == col, side, jnp.float32(0.0))

    @pl.when(half == 0)
    def _():
        d_square_ref[...] = d_ref[:, :size]
        x_square_ref[...] = x_ref[:, :size]
        side_ref[...] = side[:, size:]

    @pl.when(half == 1)
    def _():
        d_square_ref[...] = d_ref[:, size:]
        x_square_ref[...] = x_ref[:, size:]
        side_ref[...] = side[:, :size]


def first_kernel(flags, own_ref, out_ref):
    half = flags[HALF]
    size = own_ref.shape[0]
    out_ref[...] = own_ref[...] + lone_diag(flags, half * size, own_ref.shape)

    def body(step, carry):
        block = jnp.where(half == 0, step, 4 - step)
        sweep(out_ref, block, block * TILE - half * size)
        return carry

    lax.fori_loop(0, 2, body, 0)


def complete(half, own_ref, square, turned_ref, full_ref):
    size = own_ref.shape[0]
    own = own_ref[...]
    turned_ref[...] = own.T
    full_ref[rows_of(half, size), :] = own

    @pl.when(half == 0)
    def _():
        full_ref[size:, :size] = turned_ref[size:, :]
        full_ref[size:, size:] = square

    @pl.when(half == 1)
    def _():
        full_ref[:size, size:] = turned_ref[:size, :]
        full_ref[:size, :size] = square


def second_kernel(first_col, flags, own_ref, swept_ref, square_ref, out_ref, turned_ref):
    half = flags[HALF]
    size = own_ref.shape[0]
    square = square_ref[:, first_col : first_col + size]
    complete(half, own_ref, square, turned_ref, out_ref)
    other_rows = rows_of(1 - half, size)
    done_cols = pl.multiple_of(half * 384, TILE)
    column = out_ref[other_rows, pl.ds(done_cols, 256)]
    solved = swept_ref[pl.ds(pl.multiple_of(half * 64, 64), 256), :]
    shape = own_ref.shape
    lane = lax.broadcasted_iota(jnp.int32, shape, 1)
    done = (lane >= done_cols) & (lane < done_cols + 256)
    other = out_ref[other_rows, :] + lone_diag(flags, (1 - half) * size, shape)
    out_ref[rows_of(half, size), :] = swept_ref[...]
    out_ref[other_rows, :] = jnp.where(done, jnp.float32(0.0), other) - six_pass(column, solved)

    def body(step, carry):
        block = jnp.where(half == 0, 2 + step, 2 - step)
        sweep(out_ref, block, block * TILE)
        return carry

    lax.fori_loop(0, 3, body, 0)


def rest_kernel(flags, inverse_ref, x_ref, square_ref, g_ref, rest_ref, turned_ref, full_ref):
    half = flags[HALF]
    size, width = x_ref.shape
    complete(half, x_ref, square_ref[...], turned_ref, full_ref)
    g_ref[...] = factor_of(flags[LIVE]) * six_pass(full_ref[...], inverse_ref[...])
    own_rows, other_rows = rows_of(half, size), rows_of(1 - half, size)
    rest_ref[:, :width] = x_ref[...] - six_pass(g_ref[own_rows, :], full_ref[...])
    rest_ref[:, width : width + size] = square_ref[...] - six_pass(
        g_ref[other_rows, :], full_ref[other_rows, :], across=True
    )
    rest_ref[:, width + size :] = jnp.zeros_like(rest_ref[:, width + size :])


def link_kernel(
    flags, g_ref, y_ref, d_square_ref, x_square_ref, side_ref,
    link_ref, turned_link_ref, turned_ref, full_ref,
):
    size = y_ref.shape[0]
    row = lax.broadcasted_iota(jnp.int32, (size, size), 0)
    col = lax.broadcasted_iota(jnp.int32, (size, size), 1)
    side = jnp.where(row == col, side_ref[...], jnp.float32(0.0))
    y_square = (d_square_ref[...] - x_square_ref[...]) - side
    complete(flags[HALF], y_ref, y_square, turned_ref, full_ref)
    live = -factor_of(flags[LIVE_FAR])
    g = g_ref[...]
    link_ref[...] = live * three_pass(g, full_ref[...])
    turned_link_ref[...] = live * three_pass(y_ref[...], g, across=True)


def combine_kernel(flags, rest_ref, came_ref, diag_ref, link_ref, own_out, packed_out):
    size, width = own_out.shape
    row = lax.broadcasted_iota(jnp.int32, (size, width), 0) + flags[HALF] * size
    col = lax.broadcasted_iota(jnp.int32, (size, width), 1)
    own_diag = jnp.where(row == col, diag_ref[:, :width], jnp.float32(0.0))
    own_out[...] = rest_ref[:, :width] + came_ref[:, :width] + own_diag
    tail = rest_ref.shape[1] - width
    row = lax.broadcasted_iota(jnp.int32, (size, tail), 0)
    col = lax.broadcasted_iota(jnp.int32, (size, tail), 1)
    square_diag = jnp.where(row == col, diag_ref[:, width:], jnp.float32(0.0))
    packed_out[:, :width] = link_ref[...]
    packed_out[:, width:] = rest_ref[:, width:] + came_ref[:, width:] + square_diag


def near_kernel(flags, g_ref, near_ref, loads_ref, part_ref, sum_ref):
    part = three_pass(g_ref[...], near_ref[...])
    part_ref[...] = part
    sum_ref[...] = loads_ref[...] + part


def post_kernel(flags, inverse_ref, link_ref, far_ref, diag_ref, g_ref, kept_ref, sent_ref, part_ref):
    half, core = flags[HALF], flags[CORE]
    size, width = diag_ref.shape
    link = link_ref[...]
    both = three_pass(jnp.concatenate([link, far_ref[:, :width]], 0), inverse_ref[...])
    g_ref[...] = both[:width]
    left = jnp.concatenate([g_ref[rows_of(half, size), :], both[width:]], 0)
    part_ref[...] = three_pass(left, link, across=True)
    part = size // 2
    keep = pl.multiple_of(core * part, 32)
    send = pl.multiple_of((1 - core) * part, 32)
    kept_ref[:part, :] = diag_ref[pl.ds(keep, part), :] - part_ref[pl.ds(keep, part), :]
    kept_ref[part:, :] = -part_ref[pl.ds(size + keep, part), :]
    sent_ref[:part, :] = -part_ref[pl.ds(send, part), :]
    sent_ref[part:, :] = -part_ref[pl.ds(size + send, part), :]


def last_kernel(flags, g_ref, loads_ref, near_ref, kept_ref, sent_ref, part_ref):
    core = flags[CORE]
    width = kept_ref.shape[1]
    part_ref[...] = three_pass(g_ref[...], near_ref[...])
    keep = pl.ds(pl.multiple_of(core * width, width), width)
    send = pl.ds(pl.multiple_of((1 - core) * width, width), width)
    kept_ref[...] = loads_ref[:, keep] - part_ref[:, keep]
    sent_ref[...] = -part_ref[:, send]


def device(layer, half, core):
    return layer * 4 + half * 2 + core


def pairs_of(count, moves):
    pairs = []
    for layer in range(count):
        for half in range(2):
            for core, up, across, onto in moves:
                if 0 <= layer + up < count:
                    pairs.append(
                        (device(layer, half, core), device(layer + up, half ^ across, onto))
                    )
    return pairs


def after(array, *others):
    return lax.optimization_barrier((array,) + others)[0]


def shards(coupling, density, support, loads):
    part = coupling.shape[1]
    width = coupling.shape[2]
    layers = lax.axis_size("layer")
    layer = lax.axis_index("layer")
    place = lax.axis_index("rhs")
    half = place // 2
    core = place % 2
    upper = core == 1

    def move(array, *moves):
        return lax.ppermute(array, AXES, pairs_of(layers, moves))

    def straight(array, by):
        return move(array, (0, by, 0, 0), (1, -by, 0, 1))

    def crossed(array, by):
        return move(array, (1, by, 0, 0), (0, -by, 0, 1))

    def sibling(array):
        return move(array, (0, 0, 0, 1), (1, 0, 0, 0))

    def opposite(array):
        return move(array, (0, 0, 1, 0), (1, 0, 1, 1))

    def flipped(array):
        pairs = pairs_of(layers, [(1, 1, 1, 0), (0, -1, 1, 1)])
        for side in range(2):
            pairs.append((device(layers - 1, side, 1), device(layers - 1, 1 - side, 1)))
        return lax.ppermute(array, AXES, pairs)

    def pick(on_upper, on_lower):
        return jnp.where(upper, on_upper, on_lower)

    span = 2 * part
    cases = loads.shape[2]

    live = jnp.logical_not(upper & (layer == layers - 1))
    live_far = jnp.logical_not(upper & (layer == layers - 2))
    lone = jnp.logical_not(pick(layer + 2 < layers, layer >= 2))
    zero = jnp.zeros((), jnp.int32)
    flags_0 = jnp.stack([half, core, live, live_far, zero]).astype(jnp.int32)
    flags_1 = jnp.stack([half, core, live, live_far, lone]).astype(jnp.int32)
    own_shape = (span, width)
    full_shape = (width, width)
    square_shape = (span, span)
    packed_shape = (span, width + 3 * TILE)
    load_shape = (width, cases)
    pair_shape = (width, 2 * cases)
    turned_shape = (width, span)

    rho = 0.3 + 0.7 * density[0].astype(jnp.float32)
    rho_rows = lax.dynamic_slice_in_dim(rho, place * part, part, 0)
    stiff = rho_rows[:, None] * coupling[0] * rho[None, :]
    stiff = jnp.concatenate([stiff, support, jnp.ones((ROWS - 1, width), jnp.float32)], axis=0)
    far_b = move(stiff, (1, 2, 0, 0), (0, 0, 0, 1))
    far_a = move(stiff, (0, 2, 0, 0))
    near_b = crossed(stiff, 1)
    near_a = straight(stiff, 1)
    x_own, y_own, d_own, d_square, x_square, other_side = local_call(
        gather_kernel, "gather", 1, 10, flags_0, [stiff, far_a, far_b, near_a, near_b],
        [own_shape, own_shape, own_shape, square_shape, square_shape, (1, span)],
    )
    d_square = opposite(d_square)
    loads_0 = loads[0]
    loads_in = sibling(loads_0)
    loads_0 = jnp.concatenate([pick(loads_in, loads_0), pick(loads_0, loads_in)], axis=1)
    (swept_0,) = local_call(first_kernel, "invert_first", 9, 6, flags_0, [d_own], [own_shape])
    x_square = flipped(after(x_square, swept_0))
    near_loads = straight(after(loads_0, swept_0), 1)
    (inverse,) = local_call(
        functools.partial(second_kernel, 0), "invert_second", 14, 14, flags_0,
        [d_own, swept_0, d_square], [full_shape], [turned_shape],
    )
    g_full, rest = local_call(
        rest_kernel, "rest", 1, 20, flags_0, [inverse, x_own, x_square],
        [full_shape, packed_shape], [turned_shape, full_shape],
    )
    rest_in = sibling(rest)
    link, turned_link = local_call(
        link_kernel, "links", 5, 18, flags_0,
        [g_full, after(y_own, near_loads), d_square, x_square, other_side],
        [full_shape, own_shape], [turned_shape, full_shape],
    )
    other_support = jnp.where(half == 0, support[:, span:], support[:, :span])
    rest_diag = jnp.concatenate([support, other_support, jnp.zeros((1, 3 * TILE - span))], axis=1)
    new_own, packed = local_call(
        combine_kernel, "combine", 1, 10, flags_0, [rest, rest_in, rest_diag, turned_link],
        [own_shape, packed_shape],
    )
    d_own = straight(new_own, 2)
    packed = straight(packed, 2)
    near_part, new_loads = local_call(
        near_kernel, "near_loads", 2, 16, flags_0, [after(g_full, new_own), near_loads, loads_0],
        [pair_shape, pair_shape],
    )
    new_loads = new_loads + sibling(near_part)

    (swept,) = local_call(first_kernel, "invert_first", 9, 6, flags_1, [d_own], [own_shape])
    near_loads = straight(after(new_loads, swept), 2)
    (inverse,) = local_call(
        functools.partial(second_kernel, width), "invert_second", 14, 14, flags_1,
        [d_own, swept, packed], [full_shape], [turned_shape],
    )
    g_full, kept, sent = local_call(
        post_kernel, "last_blocks", 6, 22, flags_1, [inverse, link, packed, new_own],
        [full_shape, own_shape, own_shape], [full_shape],
    )
    came = sibling(sent)
    load_kept, load_sent = local_call(
        last_kernel, "last_loads", 2, 16, flags_1, [g_full, new_loads, near_loads],
        [load_shape, load_shape], [pair_shape],
    )
    loads_out = load_kept + sibling(load_sent)
    diag_out = kept[:part] + came[:part]
    lower_out = pick(came[part:], kept[part:])
    upper_out = pick(kept[part:], came[part:])
    return (diag_out[None], lower_out[None], upper_out[None], loads_out[None])


def solution(mesh):
    placed = (P("layer", "rhs", None), P("layer", None), P("layer", None), P("layer", None, "rhs"))
    return jax.shard_map(
        shards,
        mesh=mesh,
        in_specs=placed,
        out_specs=(
            P("layer", "rhs", None),
            P("layer", "rhs", None),
            P("layer", "rhs", None),
            P("layer", None, "rhs"),
        ),
        check_vma=False,
    )
```

```python
import functools

import jax
import jax.numpy as jnp
from jax import lax
from jax.experimental import pallas as pl
from jax.experimental.pallas import tpu as pltpu
from jax.sharding import PartitionSpec as P

TILE = 128
ROWS = 8
AXES = ("layer", "rhs")


def split3(x):
    high = x.astype(jnp.bfloat16)
    rest = x - high.astype(jnp.float32)
    mid = rest.astype(jnp.bfloat16)
    low = (rest - mid.astype(jnp.float32)).astype(jnp.bfloat16)
    return high, mid, low


def bdot(a, b):
    return jnp.dot(a, b, preferred_element_type=jnp.float32)


def thin_matmul(a, b):
    ah, am, al = split3(a)
    bh, bm, bl = split3(b)
    small = bdot(jnp.concatenate([ah, al], 1), jnp.concatenate([bl, bh], 0))
    mid = bdot(jnp.concatenate([ah, am], 1), jnp.concatenate([bm, bm], 0))
    top = bdot(jnp.concatenate([ah, am], 1), jnp.concatenate([bh, bh], 0))
    return top + (mid + small)


def product(a, b, across):
    dims = (((1,), (1 if across else 0,)), ((), ()))
    return lax.dot_general(a, b, dims, preferred_element_type=jnp.float32)


def six_pass(a, b, across=False):
    ah, am, al = split3(a)
    bh, bm, bl = split3(b)
    left = jnp.concatenate([al, ah, am, am, ah, ah], 1)
    right = jnp.concatenate([bh, bl, bm, bh, bm, bh], 1 if across else 0)
    return product(left, right, across)


def split2(x):
    high = x.astype(jnp.bfloat16)
    return high, (x - high.astype(jnp.float32)).astype(jnp.bfloat16)


def three_pass(a, b, across=False):
    ah, al = split2(a)
    bh, bl = split2(b)
    return product(ah, bh, across) + (product(ah, bl, across) + product(al, bh, across))


def lanes(x, j):
    return jnp.broadcast_to(x[:, j : j + 1], (ROWS, TILE))


def subs(x, j):
    return jnp.broadcast_to(x[j : j + 1, :], (ROWS, TILE))


def tree_sum(terms):
    terms = list(terms)
    while len(terms) > 1:
        terms = [sum(terms[i : i + 2][1:], terms[i]) for i in range(0, len(terms), 2)]
    return terms[0]


def short_matmul(a, b):
    ah, am, al = split3(a)
    bh, bm, bl = split3(b)
    return bdot(
        jnp.concatenate([al, ah, am, am, ah, ah], 1), jnp.concatenate([bh, bl, bm, bh, bm, bh], 0)
    )


GROUP = 2


def invert_tile(block):
    count = TILE // ROWS
    span = GROUP * ROWS
    rows = [block[ROWS * i : ROWS * i + ROWS, :] for i in range(count)]
    lane = lax.broadcasted_iota(jnp.int32, (ROWS, TILE), 1)
    sub = lax.broadcasted_iota(jnp.int32, (ROWS, TILE), 0)
    units = [jnp.where(sub == t, jnp.float32(1.0), jnp.float32(0.0)) for t in range(ROWS)]
    b = [lanes(rows[0], j) for j in range(ROWS)]
    for first in range(0, count, GROUP):
        now = list(range(first, first + GROUP))
        soon = [i for i in range(first + GROUP, first + 2 * GROUP) if i < count]
        rest = [i for i in range(count) if i not in now and i not in soon]
        before = list(rows)
        for p in now:
            k = ROWS * p
            inside = (lane >= k) & (lane < k + ROWS)
            r = rows[p]
            ahead = []
            if p + 1 < count:
                ahead = [lanes(r, k + ROWS + j) for j in range(ROWS)]
                below = [lanes(rows[p + 1], k + j) for j in range(ROWS)]
                beyond = [lanes(rows[p + 1], k + ROWS + j) for j in range(ROWS)]
            r = jnp.where(inside, jnp.where(lane - k == sub, jnp.float32(1.0), jnp.float32(0.0)), r)
            for t in range(0, ROWS, 2):
                top = subs(b[t], t)
                side = subs(b[t + 1], t)
                low = subs(b[t + 1], t + 1)
                inverse = 1.0 / (top * low - side * side)
                f = (b[t] - units[t]) * (1.0 / top)
                w = ((b[t + 1] - f * side) - units[t + 1]) * top
                g = w * inverse

                def eliminate(x, hurry=False):
                    x = x - f * subs(x, t)
                    other = subs(x, t + 1)
                    return x - ((w * other) * inverse if hurry else g * other)

                for j in range(t + 2, ROWS):
                    b[j] = eliminate(b[j], j < t + 4)
                r = eliminate(r)
                ahead = [eliminate(x) for x in ahead]
            if ahead:
                b = [
                    beyond[j] - tree_sum(below[m] * subs(ahead[j], m) for m in range(ROWS))
                    for j in range(ROWS)
                ]
            q = [subs(r, j) for j in range(ROWS)]
            for i in [i for i in now + soon if i > p] + [i for i in now if i < p]:
                e = rows[i]
                spread = below if i == p + 1 else [lanes(e, k + j) for j in range(ROWS)]
                kept = jnp.where(inside, jnp.float32(0.0), e)
                rows[i] = kept - tree_sum(spread[j] * q[j] for j in range(ROWS))
            rows[p] = r
        start = first * ROWS
        solved = jnp.concatenate([rows[i] for i in now], 0)
        for part in ([i for i in rest if i > first], [i for i in rest if i < first]):
            if part:
                c = jnp.concatenate([before[i] for i in part], 0)
                wide = lax.broadcasted_iota(jnp.int32, c.shape, 1)
                done = (wide >= start) & (wide < start + span)
                update = short_matmul(c[:, start : start + span], solved)
                c = jnp.where(done, jnp.float32(0.0), c) - update
                for m, i in enumerate(part):
                    rows[i] = c[ROWS * m : ROWS * m + ROWS, :]
    return jnp.concatenate(rows, 0)


def sweep(a_ref, block, row_start):
    col_start = pl.multiple_of(block * TILE, TILE)
    row_start = pl.multiple_of(row_start, 64)
    rows = pl.ds(row_start, TILE)
    cols = pl.ds(col_start, TILE)
    inverse = invert_tile(a_ref[rows, cols])
    solved = thin_matmul(inverse, a_ref[rows, :])
    column = a_ref[:, cols]
    a_ref[:, cols] = jnp.zeros_like(column)
    lane = lax.broadcasted_iota(jnp.int32, solved.shape, 1)
    inside = (lane >= col_start) & (lane < col_start + TILE)
    tiled = jnp.concatenate([inverse] * (solved.shape[1] // TILE), axis=1)
    solved = jnp.where(inside, tiled, solved)
    a_ref[...] = a_ref[...] - thin_matmul(column, solved)
    a_ref[rows, :] = solved


SMEM = pl.BlockSpec(memory_space=pltpu.SMEM)
VMEM = pl.BlockSpec(memory_space=pltpu.VMEM)
HALF, CORE, LIVE, LIVE_FAR, LONE = range(5)


def local_call(body, name, micros, mebibytes, flags, inputs, shapes, scratch=()):
    out = pl.pallas_call(
        body,
        out_shape=[jax.ShapeDtypeStruct(shape, jnp.float32) for shape in shapes],
        in_specs=[SMEM] + [VMEM] * len(inputs),
        out_specs=[VMEM] * len(shapes),
        scratch_shapes=[pltpu.VMEM(shape, jnp.float32) for shape in scratch],
        compiler_params=pltpu.CompilerParams(vmem_limit_bytes=mebibytes * 1024 * 1024),
        cost_estimate=pl.CostEstimate(
            flops=int(micros * 1.1e9), transcendentals=0, bytes_accessed=int(micros * 3.5e6)
        ),
        name=name,
    )(flags, *inputs)
    return out


def rows_of(half, size):
    return pl.ds(pl.multiple_of(half * size, 64), size)


def lone_diag(flags, offset, shape):
    row = lax.broadcasted_iota(jnp.int32, shape, 0) + offset
    col = lax.broadcasted_iota(jnp.int32, shape, 1)
    lone = jnp.where(flags[LONE] == 1, jnp.float32(1.0), jnp.float32(0.0))
    return jnp.where(row == col, lone, jnp.float32(0.0))


def factor_of(flag):
    return jnp.where(flag == 1, jnp.float32(1.0), jnp.float32(0.0))


def gather_kernel(
    flags, own_ref, far_a_ref, far_b_ref, near_a_ref, near_b_ref,
    x_ref, y_ref, d_ref, d_square_ref, x_square_ref, side_ref,
):
    half = flags[HALF]
    upper = flags[CORE] == 1
    size, width = x_ref.shape
    part = size // 2
    near_a, near_b = near_a_ref[:part, :], near_b_ref[:part, :]
    far_a, far_b = far_a_ref[:part, :], far_b_ref[:part, :]
    x_ref[:part, :] = jnp.where(upper, far_b, near_a)
    x_ref[part:, :] = jnp.where(upper, own_ref[:part, :], near_b)
    y_ref[:part, :] = jnp.where(upper, near_b, far_a)
    y_ref[part:, :] = jnp.where(upper, near_a, far_b)
    side = jnp.where(
        near_a_ref[part + 1 : part + 2, :] > 0.5, near_a_ref[part : part + 1, :], jnp.float32(1.0)
    )
    row = lax.broadcasted_iota(jnp.int32, (size, width), 0) + half * size
    col = lax.broadcasted_iota(jnp.int32, (size, width), 1)
    d_ref[...] = (x_ref[...] + y_ref[...]) + jnp.where(row == col, side, jnp.float32(0.0))

    @pl.when(half == 0)
    def _():
        d_square_ref[...] = d_ref[:, :size]
        x_square_ref[...] = x_ref[:, :size]
        side_ref[...] = side[:, size:]

    @pl.when(half == 1)
    def _():
        d_square_ref[...] = d_ref[:, size:]
        x_square_ref[...] = x_ref[:, size:]
        side_ref[...] = side[:, :size]


def first_kernel(flags, own_ref, out_ref):
    half = flags[HALF]
    size = own_ref.shape[0]
    out_ref[...] = own_ref[...] + lone_diag(flags, half * size, own_ref.shape)

    def body(step, carry):
        block = jnp.where(half == 0, step, 4 - step)
        sweep(out_ref, block, block * TILE - half * size)
        return carry

    lax.fori_loop(0, 2, body, 0)


def complete(half, own_ref, square, turned_ref, full_ref):
    size = own_ref.shape[0]
    own = own_ref[...]
    turned_ref[...] = own.T
    full_ref[rows_of(half, size), :] = own

    @pl.when(half == 0)
    def _():
        full_ref[size:, :size] = turned_ref[size:, :]
        full_ref[size:, size:] = square

    @pl.when(half == 1)
    def _():
        full_ref[:size, size:] = turned_ref[:size, :]
        full_ref[:size, :size] = square


def second_kernel(first_col, flags, own_ref, swept_ref, square_ref, out_ref, turned_ref):
    half = flags[HALF]
    size = own_ref.shape[0]
    square = square_ref[:, first_col : first_col + size]
    complete(half, own_ref, square, turned_ref, out_ref)
    other_rows = rows_of(1 - half, size)
    done_cols = pl.multiple_of(half * 384, TILE)
    column = out_ref[other_rows, pl.ds(done_cols, 256)]
    solved = swept_ref[pl.ds(pl.multiple_of(half * 64, 64), 256), :]
    shape = own_ref.shape
    lane = lax.broadcasted_iota(jnp.int32, shape, 1)
    done = (lane >= done_cols) & (lane < done_cols + 256)
    other = out_ref[other_rows, :] + lone_diag(flags, (1 - half) * size, shape)
    out_ref[rows_of(half, size), :] = swept_ref[...]
    out_ref[other_rows, :] = jnp.where(done, jnp.float32(0.0), other) - six_pass(column, solved)

    def body(step, carry):
        block = jnp.where(half == 0, 2 + step, 2 - step)
        sweep(out_ref, block, block * TILE)
        return carry

    lax.fori_loop(0, 3, body, 0)


def rest_kernel(flags, inverse_ref, x_ref, square_ref, g_ref, rest_ref, turned_ref, full_ref):
    half = flags[HALF]
    size, width = x_ref.shape
    complete(half, x_ref, square_ref[...], turned_ref, full_ref)
    g_ref[...] = factor_of(flags[LIVE]) * six_pass(full_ref[...], inverse_ref[...])
    own_rows, other_rows = rows_of(half, size), rows_of(1 - half, size)
    rest_ref[:, :width] = x_ref[...] - six_pass(g_ref[own_rows, :], full_ref[...])
    rest_ref[:, width : width + size] = square_ref[...] - six_pass(
        g_ref[other_rows, :], full_ref[other_rows, :], across=True
    )
    rest_ref[:, width + size :] = jnp.zeros_like(rest_ref[:, width + size :])


def link_kernel(
    flags, g_ref, y_ref, y_square_ref, link_ref, turned_link_ref, turned_ref, full_ref
):
    complete(flags[HALF], y_ref, y_square_ref[...], turned_ref, full_ref)
    live = -factor_of(flags[LIVE_FAR])
    g = g_ref[...]
    link_ref[...] = live * three_pass(g, full_ref[...])
    turned_link_ref[...] = live * three_pass(y_ref[...], g, across=True)


def combine_kernel(flags, rest_ref, came_ref, diag_ref, link_ref, own_out, packed_out):
    size, width = own_out.shape
    row = lax.broadcasted_iota(jnp.int32, (size, width), 0) + flags[HALF] * size
    col = lax.broadcasted_iota(jnp.int32, (size, width), 1)
    own_diag = jnp.where(row == col, diag_ref[:, :width], jnp.float32(0.0))
    own_out[...] = rest_ref[:, :width] + came_ref[:, :width] + own_diag
    tail = rest_ref.shape[1] - width
    row = lax.broadcasted_iota(jnp.int32, (size, tail), 0)
    col = lax.broadcasted_iota(jnp.int32, (size, tail), 1)
    square_diag = jnp.where(row == col, diag_ref[:, width:], jnp.float32(0.0))
    packed_out[:, :width] = link_ref[...]
    packed_out[:, width:] = rest_ref[:, width:] + came_ref[:, width:] + square_diag


def near_kernel(flags, g_ref, near_ref, part_ref):
    part_ref[...] = three_pass(g_ref[...], near_ref[...])


def post_kernel(flags, inverse_ref, link_ref, far_ref, diag_ref, g_ref, kept_ref, sent_ref, part_ref):
    half, core = flags[HALF], flags[CORE]
    size, width = diag_ref.shape
    link = link_ref[...]
    both = three_pass(jnp.concatenate([link, far_ref[:, :width]], 0), inverse_ref[...])
    g_ref[...] = both[:width]
    left = jnp.concatenate([g_ref[rows_of(half, size), :], both[width:]], 0)
    part_ref[...] = three_pass(left, link, across=True)
    part = size // 2
    keep = pl.multiple_of(core * part, 32)
    send = pl.multiple_of((1 - core) * part, 32)
    kept_ref[:part, :] = diag_ref[pl.ds(keep, part), :] - part_ref[pl.ds(keep, part), :]
    kept_ref[part:, :] = -part_ref[pl.ds(size + keep, part), :]
    sent_ref[:part, :] = -part_ref[pl.ds(send, part), :]
    sent_ref[part:, :] = -part_ref[pl.ds(size + send, part), :]


def last_kernel(flags, g_ref, loads_ref, near_ref, kept_ref, sent_ref, part_ref):
    core = flags[CORE]
    width = kept_ref.shape[1]
    part_ref[...] = three_pass(g_ref[...], near_ref[...])
    keep = pl.ds(pl.multiple_of(core * width, width), width)
    send = pl.ds(pl.multiple_of((1 - core) * width, width), width)
    kept_ref[...] = loads_ref[:, keep] - part_ref[:, keep]
    sent_ref[...] = -part_ref[:, send]


def device(layer, half, core):
    return layer * 4 + half * 2 + core


def pairs_of(count, moves):
    pairs = []
    for layer in range(count):
        for half in range(2):
            for core, up, across, onto in moves:
                if 0 <= layer + up < count:
                    pairs.append(
                        (device(layer, half, core), device(layer + up, half ^ across, onto))
                    )
    return pairs


def after(array, *others):
    return lax.optimization_barrier((array,) + others)[0]


def shards(coupling, density, support, loads):
    part = coupling.shape[1]
    width = coupling.shape[2]
    layers = lax.axis_size("layer")
    layer = lax.axis_index("layer")
    place = lax.axis_index("rhs")
    half = place // 2
    core = place % 2
    upper = core == 1

    def move(array, *moves):
        return lax.ppermute(array, AXES, pairs_of(layers, moves))

    def straight(array, by):
        return move(array, (0, by, 0, 0), (1, -by, 0, 1))

    def crossed(array, by):
        return move(array, (1, by, 0, 0), (0, -by, 0, 1))

    def sibling(array):
        return move(array, (0, 0, 0, 1), (1, 0, 0, 0))

    def opposite(array):
        return move(array, (0, 0, 1, 0), (1, 0, 1, 1))

    def flipped(array):
        pairs = pairs_of(layers, [(1, 1, 1, 0), (0, -1, 1, 1)])
        for side in range(2):
            pairs.append((device(layers - 1, side, 1), device(layers - 1, 1 - side, 1)))
        return lax.ppermute(array, AXES, pairs)

    def pick(on_upper, on_lower):
        return jnp.where(upper, on_upper, on_lower)

    span = 2 * part
    cases = loads.shape[2]

    live = jnp.logical_not(upper & (layer == layers - 1))
    live_far = jnp.logical_not(upper & (layer == layers - 2))
    lone = jnp.logical_not(pick(layer + 2 < layers, layer >= 2))
    zero = jnp.zeros((), jnp.int32)
    flags_0 = jnp.stack([half, core, live, live_far, zero]).astype(jnp.int32)
    flags_1 = jnp.stack([half, core, live, live_far, lone]).astype(jnp.int32)
    own_shape = (span, width)
    full_shape = (width, width)
    square_shape = (span, span)
    packed_shape = (span, width + 3 * TILE)
    load_shape = (width, cases)
    pair_shape = (width, 2 * cases)
    turned_shape = (width, span)

    rho = 0.3 + 0.7 * density[0].astype(jnp.float32)
    rho_rows = lax.dynamic_slice_in_dim(rho, place * part, part, 0)
    stiff = rho_rows[:, None] * coupling[0] * rho[None, :]
    stiff = jnp.concatenate([stiff, support, jnp.ones((ROWS - 1, width), jnp.float32)], axis=0)
    far_b = move(stiff, (1, 2, 0, 0), (0, 0, 0, 1))
    far_a = move(stiff, (0, 2, 0, 0))
    near_b = crossed(stiff, 1)
    near_a = straight(stiff, 1)
    x_own, y_own, d_own, d_square, x_square, other_side = local_call(
        gather_kernel, "gather", 1, 10, flags_0, [stiff, far_a, far_b, near_a, near_b],
        [own_shape, own_shape, own_shape, square_shape, square_shape, (1, span)],
    )
    d_square = opposite(d_square)
    loads_0 = loads[0]
    loads_in = sibling(loads_0)
    loads_0 = jnp.concatenate([pick(loads_in, loads_0), pick(loads_0, loads_in)], axis=1)
    (swept_0,) = local_call(first_kernel, "invert_first", 9, 6, flags_0, [d_own], [own_shape])
    x_square = flipped(after(x_square, swept_0))
    near_loads = straight(after(loads_0, swept_0), 1)
    (inverse,) = local_call(
        functools.partial(second_kernel, 0), "invert_second", 14, 14, flags_0,
        [d_own, swept_0, d_square], [full_shape], [turned_shape],
    )
    row = lax.broadcasted_iota(jnp.int32, square_shape, 0)
    col = lax.broadcasted_iota(jnp.int32, square_shape, 1)
    y_square = (d_square - x_square) - jnp.where(row == col, other_side, jnp.float32(0.0))
    g_full, rest = local_call(
        rest_kernel, "rest", 1, 28, flags_0, [inverse, x_own, x_square],
        [full_shape, packed_shape], [turned_shape, full_shape],
    )
    rest_in = sibling(rest)
    link, turned_link = local_call(
        link_kernel, "links", 5, 18, flags_0,
        [g_full, after(y_own, near_loads), y_square],
        [full_shape, own_shape], [turned_shape, full_shape],
    )
    other_support = jnp.where(half == 0, support[:, span:], support[:, :span])
    rest_diag = jnp.concatenate([support, other_support, jnp.zeros((1, 3 * TILE - span))], axis=1)
    new_own, packed = local_call(
        combine_kernel, "combine", 1, 10, flags_0, [rest, rest_in, rest_diag, turned_link],
        [own_shape, packed_shape],
    )
    d_own = straight(new_own, 2)
    packed = straight(packed, 2)
    (near_part,) = local_call(
        near_kernel, "near_loads", 2, 16, flags_0, [after(g_full, new_own), near_loads], [pair_shape]
    )
    new_loads = loads_0 + near_part + sibling(near_part)

    (swept,) = local_call(first_kernel, "invert_first", 9, 6, flags_1, [d_own], [own_shape])
    near_loads = straight(after(new_loads, swept), 2)
    (inverse,) = local_call(
        functools.partial(second_kernel, width), "invert_second", 14, 14, flags_1,
        [d_own, swept, packed], [full_shape], [turned_shape],
    )
    g_full, kept, sent = local_call(
        post_kernel, "last_blocks", 6, 22, flags_1, [inverse, link, packed, new_own],
        [full_shape, own_shape, own_shape], [full_shape],
    )
    came = sibling(sent)
    load_kept, load_sent = local_call(
        last_kernel, "last_loads", 2, 16, flags_1, [g_full, new_loads, near_loads],
        [load_shape, load_shape], [pair_shape],
    )
    loads_out = load_kept + sibling(load_sent)
    diag_out = kept[:part] + came[:part]
    lower_out = pick(came[part:], kept[part:])
    upper_out = pick(kept[part:], came[part:])
    return (diag_out[None], lower_out[None], upper_out[None], loads_out[None])


def solution(mesh):
    placed = (P("layer", "rhs", None), P("layer", None), P("layer", None), P("layer", None, "rhs"))
    return jax.shard_map(
        shards,
        mesh=mesh,
        in_specs=placed,
        out_specs=(
            P("layer", "rhs", None),
            P("layer", "rhs", None),
            P("layer", "rhs", None),
            P("layer", None, "rhs"),
        ),
        check_vma=False,
    )
```

```python
import functools

import jax
import jax.numpy as jnp
from jax import lax
from jax.experimental import pallas as pl
from jax.experimental.pallas import tpu as pltpu
from jax.sharding import PartitionSpec as P

TILE = 128
ROWS = 8
AXES = ("layer", "rhs")
VMEM_BYTES = 28 * 1024 * 1024


def split3(x):
    high = x.astype(jnp.bfloat16)
    rest = x - high.astype(jnp.float32)
    mid = rest.astype(jnp.bfloat16)
    low = (rest - mid.astype(jnp.float32)).astype(jnp.bfloat16)
    return high, mid, low


def bdot(a, b):
    return jnp.dot(a, b, preferred_element_type=jnp.float32)


def thin_matmul(a, b):
    ah, am, al = split3(a)
    bh, bm, bl = split3(b)
    small = bdot(jnp.concatenate([ah, al], 1), jnp.concatenate([bl, bh], 0))
    mid = bdot(jnp.concatenate([ah, am], 1), jnp.concatenate([bm, bm], 0))
    top = bdot(jnp.concatenate([ah, am], 1), jnp.concatenate([bh, bh], 0))
    return top + (mid + small)


def six_pass(a, b, across=False):
    ah, am, al = split3(a)
    bh, bm, bl = split3(b)
    left = jnp.concatenate([al, ah, am, am, ah, ah], 1)
    side = 1 if across else 0
    right = jnp.concatenate([bh, bl, bm, bh, bm, bh], side)
    return lax.dot_general(
        left, right, (((1,), (side,)), ((), ())), preferred_element_type=jnp.float32
    )


def split2(x):
    high = x.astype(jnp.bfloat16)
    return high, (x - high.astype(jnp.float32)).astype(jnp.bfloat16)


def three_pass(a, b, across=False):
    ah, al = split2(a)
    bh, bl = split2(b)
    left = jnp.concatenate([al, ah, ah], 1)
    side = 1 if across else 0
    right = jnp.concatenate([bh, bl, bh], side)
    return lax.dot_general(
        left, right, (((1,), (side,)), ((), ())), preferred_element_type=jnp.float32
    )


def lanes(x, j):
    return jnp.broadcast_to(x[:, j : j + 1], (ROWS, TILE))


def subs(x, j):
    return jnp.broadcast_to(x[j : j + 1, :], (ROWS, TILE))


def tree_sum(terms):
    terms = list(terms)
    while len(terms) > 1:
        terms = [sum(terms[i : i + 2][1:], terms[i]) for i in range(0, len(terms), 2)]
    return terms[0]


def short_matmul(a, b):
    ah, am, al = split3(a)
    bh, bm, bl = split3(b)
    return bdot(
        jnp.concatenate([al, ah, am, am, ah, ah], 1), jnp.concatenate([bh, bl, bm, bh, bm, bh], 0)
    )


GROUP = 2


def invert_tile(block):
    count = TILE // ROWS
    span = GROUP * ROWS
    rows = [block[ROWS * i : ROWS * i + ROWS, :] for i in range(count)]
    lane = lax.broadcasted_iota(jnp.int32, (ROWS, TILE), 1)
    sub = lax.broadcasted_iota(jnp.int32, (ROWS, TILE), 0)
    units = [jnp.where(sub == t, jnp.float32(1.0), jnp.float32(0.0)) for t in range(ROWS)]
    b = [lanes(rows[0], j) for j in range(ROWS)]
    for first in range(0, count, GROUP):
        now = list(range(first, first + GROUP))
        soon = [i for i in range(first + GROUP, first + 2 * GROUP) if i < count]
        rest = [i for i in range(count) if i not in now and i not in soon]
        before = list(rows)
        for p in now:
            k = ROWS * p
            inside = (lane >= k) & (lane < k + ROWS)
            r = rows[p]
            ahead = []
            if p + 1 < count:
                ahead = [lanes(r, k + ROWS + j) for j in range(ROWS)]
                below = [lanes(rows[p + 1], k + j) for j in range(ROWS)]
                beyond = [lanes(rows[p + 1], k + ROWS + j) for j in range(ROWS)]
            r = jnp.where(inside, jnp.where(lane - k == sub, jnp.float32(1.0), jnp.float32(0.0)), r)
            for t in range(0, ROWS, 2):
                top = subs(b[t], t)
                side = subs(b[t + 1], t)
                low = subs(b[t + 1], t + 1)
                inverse = 1.0 / (top * low - side * side)
                f = (b[t] - units[t]) * (1.0 / top)
                w = ((b[t + 1] - f * side) - units[t + 1]) * top
                g = w * inverse

                def eliminate(x, hurry=False):
                    x = x - f * subs(x, t)
                    other = subs(x, t + 1)
                    return x - ((w * other) * inverse if hurry else g * other)

                for j in range(t + 2, ROWS):
                    b[j] = eliminate(b[j], j < t + 4)
                r = eliminate(r)
                ahead = [eliminate(x) for x in ahead]
            if ahead:
                b = [
                    beyond[j] - tree_sum(below[m] * subs(ahead[j], m) for m in range(ROWS))
                    for j in range(ROWS)
                ]
            q = [subs(r, j) for j in range(ROWS)]
            for i in [i for i in now + soon if i > p] + [i for i in now if i < p]:
                e = rows[i]
                spread = below if i == p + 1 else [lanes(e, k + j) for j in range(ROWS)]
                kept = jnp.where(inside, jnp.float32(0.0), e)
                rows[i] = kept - tree_sum(spread[j] * q[j] for j in range(ROWS))
            rows[p] = r
        start = first * ROWS
        solved = jnp.concatenate([rows[i] for i in now], 0)
        for part in ([i for i in rest if i > first], [i for i in rest if i < first]):
            if part:
                c = jnp.concatenate([before[i] for i in part], 0)
                wide = lax.broadcasted_iota(jnp.int32, c.shape, 1)
                done = (wide >= start) & (wide < start + span)
                update = short_matmul(c[:, start : start + span], solved)
                c = jnp.where(done, jnp.float32(0.0), c) - update
                for m, i in enumerate(part):
                    rows[i] = c[ROWS * m : ROWS * m + ROWS, :]
    return jnp.concatenate(rows, 0)


def sweep(a_ref, block, row_start):
    col_start = pl.multiple_of(block * TILE, TILE)
    row_start = pl.multiple_of(row_start, 64)
    rows = pl.ds(row_start, TILE)
    cols = pl.ds(col_start, TILE)
    inverse = invert_tile(a_ref[rows, cols])
    solved = thin_matmul(inverse, a_ref[rows, :])
    column = a_ref[:, cols]
    a_ref[:, cols] = jnp.zeros_like(column)
    lane = lax.broadcasted_iota(jnp.int32, solved.shape, 1)
    inside = (lane >= col_start) & (lane < col_start + TILE)
    tiled = jnp.concatenate([inverse] * (solved.shape[1] // TILE), axis=1)
    solved = jnp.where(inside, tiled, solved)
    a_ref[...] = a_ref[...] - thin_matmul(column, solved)
    a_ref[rows, :] = solved


SMEM = pl.BlockSpec(memory_space=pltpu.SMEM)
VMEM = pl.BlockSpec(memory_space=pltpu.VMEM)
HALF, CORE, LIVE, LIVE_FAR, LONE = range(5)


def local_call(body, name, micros, flags, inputs, shapes, scratch=()):
    out = pl.pallas_call(
        body,
        out_shape=[jax.ShapeDtypeStruct(shape, jnp.float32) for shape in shapes],
        in_specs=[SMEM] + [VMEM] * len(inputs),
        out_specs=[VMEM] * len(shapes),
        scratch_shapes=[pltpu.VMEM(shape, jnp.float32) for shape in scratch],
        compiler_params=pltpu.CompilerParams(vmem_limit_bytes=VMEM_BYTES),
        cost_estimate=pl.CostEstimate(
            flops=int(micros * 1.1e9), transcendentals=0, bytes_accessed=int(micros * 3.5e6)
        ),
        name=name,
    )(flags, *inputs)
    return out


def rows_of(half, size):
    return pl.ds(pl.multiple_of(half * size, 64), size)


def lone_diag(flags, offset, shape):
    row = lax.broadcasted_iota(jnp.int32, shape, 0) + offset
    col = lax.broadcasted_iota(jnp.int32, shape, 1)
    lone = jnp.where(flags[LONE] == 1, jnp.float32(1.0), jnp.float32(0.0))
    return jnp.where(row == col, lone, jnp.float32(0.0))


def factor_of(flag):
    return jnp.where(flag == 1, jnp.float32(1.0), jnp.float32(0.0))


def first_kernel(flags, own_ref, out_ref):
    half = flags[HALF]
    size = own_ref.shape[0]
    out_ref[...] = own_ref[...] + lone_diag(flags, half * size, own_ref.shape)

    def body(step, carry):
        block = jnp.where(half == 0, step, 4 - step)
        sweep(out_ref, block, block * TILE - half * size)
        return carry

    lax.fori_loop(0, 2, body, 0)


def complete(half, own_ref, square, turned_ref, full_ref):
    size = own_ref.shape[0]
    own = own_ref[...]
    turned_ref[...] = own.T
    full_ref[rows_of(half, size), :] = own

    @pl.when(half == 0)
    def _():
        full_ref[size:, :size] = turned_ref[size:, :]
        full_ref[size:, size:] = square

    @pl.when(half == 1)
    def _():
        full_ref[:size, size:] = turned_ref[:size, :]
        full_ref[:size, :size] = square


def second_kernel(first_col, flags, own_ref, swept_ref, square_ref, out_ref, turned_ref):
    half = flags[HALF]
    size = own_ref.shape[0]
    square = square_ref[:, first_col : first_col + size]
    complete(half, own_ref, square, turned_ref, out_ref)
    other_rows = rows_of(1 - half, size)
    done_cols = pl.multiple_of(half * 384, TILE)
    column = out_ref[other_rows, pl.ds(done_cols, 256)]
    solved = swept_ref[pl.ds(pl.multiple_of(half * 64, 64), 256), :]
    shape = own_ref.shape
    lane = lax.broadcasted_iota(jnp.int32, shape, 1)
    done = (lane >= done_cols) & (lane < done_cols + 256)
    other = out_ref[other_rows, :] + lone_diag(flags, (1 - half) * size, shape)
    out_ref[rows_of(half, size), :] = swept_ref[...]
    out_ref[other_rows, :] = jnp.where(done, jnp.float32(0.0), other) - six_pass(column, solved)

    def body(step, carry):
        block = jnp.where(half == 0, 2 + step, 2 - step)
        sweep(out_ref, block, block * TILE)
        return carry

    lax.fori_loop(0, 3, body, 0)


def rest_kernel(flags, inverse_ref, x_ref, square_ref, g_ref, rest_ref, turned_ref, full_ref):
    half = flags[HALF]
    size, width = x_ref.shape
    complete(half, x_ref, square_ref[...], turned_ref, full_ref)
    g_ref[...] = factor_of(flags[LIVE]) * six_pass(full_ref[...], inverse_ref[...])
    own_rows, other_rows = rows_of(half, size), rows_of(1 - half, size)
    rest_ref[:, :width] = x_ref[...] - six_pass(g_ref[own_rows, :], full_ref[...])
    rest_ref[:, width : width + size] = square_ref[...] - six_pass(
        g_ref[other_rows, :], full_ref[other_rows, :], across=True
    )
    rest_ref[:, width + size :] = jnp.zeros_like(rest_ref[:, width + size :])


def link_kernel(flags, g_ref, y_ref, y_square_ref, link_ref, turned_link_ref, turned_ref, full_ref):
    complete(flags[HALF], y_ref, y_square_ref[...], turned_ref, full_ref)
    live = -factor_of(flags[LIVE_FAR])
    g = g_ref[...]
    link_ref[...] = live * three_pass(g, full_ref[...])
    turned_link_ref[...] = live * three_pass(y_ref[...], g, across=True)


def combine_kernel(flags, rest_ref, came_ref, diag_ref, link_ref, own_out, packed_out):
    size, width = own_out.shape
    row = lax.broadcasted_iota(jnp.int32, (size, width), 0) + flags[HALF] * size
    col = lax.broadcasted_iota(jnp.int32, (size, width), 1)
    own_diag = jnp.where(row == col, diag_ref[:, :width], jnp.float32(0.0))
    own_out[...] = rest_ref[:, :width] + came_ref[:, :width] + own_diag
    tail = rest_ref.shape[1] - width
    row = lax.broadcasted_iota(jnp.int32, (size, tail), 0)
    col = lax.broadcasted_iota(jnp.int32, (size, tail), 1)
    square_diag = jnp.where(row == col, diag_ref[:, width:], jnp.float32(0.0))
    packed_out[:, :width] = link_ref[...]
    packed_out[:, width:] = rest_ref[:, width:] + came_ref[:, width:] + square_diag


def near_kernel(flags, g_ref, loads_ref, part_ref):
    part_ref[...] = three_pass(g_ref[...], loads_ref[...])


def post_kernel(flags, inverse_ref, link_ref, far_ref, diag_ref, g_ref, kept_ref, sent_ref, part_ref):
    half, core = flags[HALF], flags[CORE]
    size, width = diag_ref.shape
    link = link_ref[...]
    both = three_pass(jnp.concatenate([link, far_ref[:, :width]], 0), inverse_ref[...])
    g_ref[...] = both[:width]
    left = jnp.concatenate([g_ref[rows_of(half, size), :], both[width:]], 0)
    part_ref[...] = three_pass(left, link, across=True)
    part = size // 2
    keep = pl.multiple_of(core * part, 32)
    send = pl.multiple_of((1 - core) * part, 32)
    kept_ref[:part, :] = diag_ref[pl.ds(keep, part), :] - part_ref[pl.ds(keep, part), :]
    kept_ref[part:, :] = -part_ref[pl.ds(size + keep, part), :]
    sent_ref[:part, :] = -part_ref[pl.ds(send, part), :]
    sent_ref[part:, :] = -part_ref[pl.ds(size + send, part), :]


def last_kernel(flags, g_ref, loads_ref, near_ref, kept_ref, sent_ref, part_ref):
    core = flags[CORE]
    width = kept_ref.shape[1]
    part_ref[...] = three_pass(g_ref[...], near_ref[...])
    keep = pl.ds(pl.multiple_of(core * width, width), width)
    send = pl.ds(pl.multiple_of((1 - core) * width, width), width)
    kept_ref[...] = loads_ref[:, keep] - part_ref[:, keep]
    sent_ref[...] = -part_ref[:, send]


def device(layer, half, core):
    return layer * 4 + half * 2 + core


def pairs_of(count, moves):
    pairs = []
    for layer in range(count):
        for half in range(2):
            for core, up, across, onto in moves:
                if 0 <= layer + up < count:
                    pairs.append(
                        (device(layer, half, core), device(layer + up, half ^ across, onto))
                    )
    return pairs


def after(array, *others):
    return lax.optimization_barrier((array,) + others)[0]


def shards(coupling, density, support, loads):
    part = coupling.shape[1]
    width = coupling.shape[2]
    layers = lax.axis_size("layer")
    layer = lax.axis_index("layer")
    place = lax.axis_index("rhs")
    half = place // 2
    core = place % 2
    upper = core == 1

    def move(array, *moves):
        return lax.ppermute(array, AXES, pairs_of(layers, moves))

    def straight(array, by):
        return move(array, (0, by, 0, 0), (1, -by, 0, 1))

    def crossed(array, by):
        return move(array, (1, by, 0, 0), (0, -by, 0, 1))

    def sibling(array):
        return move(array, (0, 0, 0, 1), (1, 0, 0, 0))

    def opposite(array):
        return move(array, (0, 0, 1, 0), (1, 0, 1, 1))

    def flipped(array):
        pairs = pairs_of(layers, [(1, 1, 1, 0), (0, -1, 1, 1)])
        for side in range(2):
            pairs.append((device(layers - 1, side, 1), device(layers - 1, 1 - side, 1)))
        return lax.ppermute(array, AXES, pairs)

    def pick(on_upper, on_lower):
        return jnp.where(upper, on_upper, on_lower)

    span = 2 * part
    cases = loads.shape[2]

    def square(array, first):
        return jnp.where(first == 0, array[:, :span], array[:, span:])

    live = jnp.logical_not(upper & (layer == layers - 1))
    live_far = jnp.logical_not(upper & (layer == layers - 2))
    lone = jnp.logical_not(pick(layer + 2 < layers, layer >= 2))
    zero = jnp.zeros((), jnp.int32)
    flags_0 = jnp.stack([half, core, live, live_far, zero]).astype(jnp.int32)
    flags_1 = jnp.stack([half, core, live, live_far, lone]).astype(jnp.int32)
    row = lax.broadcasted_iota(jnp.int32, (span, width), 0)
    col = lax.broadcasted_iota(jnp.int32, (span, width), 1)
    own_diag = col == row + half * span
    square_diag = row[:, :span] == col[:, :span]

    rho = 0.3 + 0.7 * density[0].astype(jnp.float32)
    rho_rows = lax.dynamic_slice_in_dim(rho, place * part, part, 0)
    stiff = rho_rows[:, None] * coupling[0] * rho[None, :]
    ones = jnp.ones((ROWS - 1, width), jnp.float32)
    tagged = jnp.concatenate([stiff, support, ones], axis=0)

    near_a = straight(tagged, 1)
    near_b = crossed(stiff, 1)
    far_a = move(stiff, (0, 2, 0, 0))
    far_b = move(stiff, (1, 2, 0, 0), (0, 0, 0, 1))
    side_support = jnp.where(near_a[part + 1] > 0.5, near_a[part], jnp.float32(1.0))
    near_a = near_a[:part]
    x_own = jnp.concatenate([pick(far_b, near_a), pick(stiff, near_b)], axis=0)
    y_own = jnp.concatenate([pick(near_b, far_a), pick(near_a, far_b)], axis=0)
    d_own = (x_own + y_own) + jnp.where(own_diag, side_support[None, :], jnp.float32(0.0))

    d_square = opposite(square(d_own, half))
    own_shape = (span, width)
    full_shape = (width, width)
    packed_shape = (span, width + 3 * TILE)
    load_shape = (width, cases)
    pair_shape = (width, 2 * cases)
    turned_shape = (width, span)

    loads_0 = loads[0]
    loads_in = sibling(loads_0)
    loads_0 = jnp.concatenate([pick(loads_in, loads_0), pick(loads_0, loads_in)], axis=1)
    (swept_0,) = local_call(first_kernel, "invert_first", 9, flags_0, [d_own], [own_shape])
    x_square = flipped(after(square(x_own, half), swept_0))
    near_loads = straight(after(loads_0, swept_0), 1)
    (inverse,) = local_call(
        functools.partial(second_kernel, 0), "invert_second", 14, flags_0,
        [d_own, swept_0, d_square], [full_shape], [turned_shape],
    )
    g_full, rest = local_call(
        rest_kernel, "rest", 1, flags_0, [inverse, x_own, x_square],
        [full_shape, packed_shape], [turned_shape, full_shape],
    )
    rest_in = sibling(rest)
    other_side = jnp.where(half == 0, side_support[span:], side_support[:span])
    y_square = (d_square - x_square) - jnp.where(square_diag, other_side[None, :], jnp.float32(0.0))
    link, turned_link = local_call(
        link_kernel, "links", 5, flags_0, [g_full, after(y_own, near_loads), y_square],
        [full_shape, own_shape], [turned_shape, full_shape],
    )
    other_support = jnp.where(half == 0, support[:, span:], support[:, :span])
    rest_diag = jnp.concatenate([support, other_support, jnp.zeros((1, 3 * TILE - span))], axis=1)
    new_own, packed = local_call(
        combine_kernel, "combine", 1, flags_0, [rest, rest_in, rest_diag, turned_link],
        [own_shape, packed_shape],
    )
    d_own = straight(new_own, 2)
    packed = straight(packed, 2)
    (near_part,) = local_call(
        near_kernel, "near_loads", 2, flags_0, [after(g_full, new_own), near_loads], [pair_shape]
    )
    new_loads = loads_0 + near_part + sibling(near_part)

    (swept,) = local_call(first_kernel, "invert_first", 9, flags_1, [d_own], [own_shape])
    near_loads = straight(after(new_loads, swept), 2)
    (inverse,) = local_call(
        functools.partial(second_kernel, width), "invert_second", 14, flags_1,
        [d_own, swept, packed], [full_shape], [turned_shape],
    )
    g_full, kept, sent = local_call(
        post_kernel, "last_blocks", 6, flags_1, [inverse, link, packed, new_own],
        [full_shape, own_shape, own_shape], [full_shape],
    )
    came = sibling(sent)
    load_kept, load_sent = local_call(
        last_kernel, "last_loads", 2, flags_1, [g_full, new_loads, near_loads],
        [load_shape, load_shape], [pair_shape],
    )
    loads_out = load_kept + sibling(load_sent)
    diag_out = kept[:part] + came[:part]
    lower_out = pick(came[part:], kept[part:])
    upper_out = pick(kept[part:], came[part:])
    return (diag_out[None], lower_out[None], upper_out[None], loads_out[None])


def solution(mesh):
    placed = (P("layer", "rhs", None), P("layer", None), P("layer", None), P("layer", None, "rhs"))
    return jax.shard_map(
        shards,
        mesh=mesh,
        in_specs=placed,
        out_specs=(
            P("layer", "rhs", None),
            P("layer", "rhs", None),
            P("layer", "rhs", None),
            P("layer", None, "rhs"),
        ),
        check_vma=False,
    )
```

```python
import functools

import jax
import jax.numpy as jnp
from jax import lax
from jax.experimental import pallas as pl
from jax.experimental.pallas import tpu as pltpu
from jax.sharding import PartitionSpec as P

TILE = 128
ROWS = 8
AXES = ("layer", "rhs")
VMEM_BYTES = 28 * 1024 * 1024


def split3(x):
    high = x.astype(jnp.bfloat16)
    rest = x - high.astype(jnp.float32)
    mid = rest.astype(jnp.bfloat16)
    low = (rest - mid.astype(jnp.float32)).astype(jnp.bfloat16)
    return high, mid, low


def bdot(a, b):
    return jnp.dot(a, b, preferred_element_type=jnp.float32)


def thin_matmul(a, b):
    ah, am, al = split3(a)
    bh, bm, bl = split3(b)
    small = bdot(jnp.concatenate([ah, al], 1), jnp.concatenate([bl, bh], 0))
    mid = bdot(jnp.concatenate([ah, am], 1), jnp.concatenate([bm, bm], 0))
    top = bdot(jnp.concatenate([ah, am], 1), jnp.concatenate([bh, bh], 0))
    return top + (mid + small)


def six_pass(a, b, across=False):
    ah, am, al = split3(a)
    bh, bm, bl = split3(b)
    left = jnp.concatenate([al, ah, am, am, ah, ah], 1)
    side = 1 if across else 0
    right = jnp.concatenate([bh, bl, bm, bh, bm, bh], side)
    return lax.dot_general(
        left, right, (((1,), (side,)), ((), ())), preferred_element_type=jnp.float32
    )


def split2(x):
    high = x.astype(jnp.bfloat16)
    return high, (x - high.astype(jnp.float32)).astype(jnp.bfloat16)


def three_pass(a, b, across=False):
    ah, al = split2(a)
    bh, bl = split2(b)
    left = jnp.concatenate([al, ah, ah], 1)
    side = 1 if across else 0
    right = jnp.concatenate([bh, bl, bh], side)
    return lax.dot_general(
        left, right, (((1,), (side,)), ((), ())), preferred_element_type=jnp.float32
    )


def parted_three_pass(a, b, across=False):
    dims = (((1,), (1 if across else 0,)), ((), ()))

    def product(left, right):
        return lax.dot_general(left, right, dims, preferred_element_type=jnp.float32)

    ah, al = split2(a)
    bh, bl = split2(b)
    return product(ah, bh) + (product(ah, bl) + product(al, bh))


def lanes(x, j):
    return jnp.broadcast_to(x[:, j : j + 1], (ROWS, TILE))


def subs(x, j):
    return jnp.broadcast_to(x[j : j + 1, :], (ROWS, TILE))


def tree_sum(terms):
    terms = list(terms)
    while len(terms) > 1:
        terms = [sum(terms[i : i + 2][1:], terms[i]) for i in range(0, len(terms), 2)]
    return terms[0]


def short_matmul(a, b):
    ah, am, al = split3(a)
    bh, bm, bl = split3(b)
    return bdot(
        jnp.concatenate([al, ah, am, am, ah, ah], 1), jnp.concatenate([bh, bl, bm, bh, bm, bh], 0)
    )


GROUP = 2


def invert_tile(block):
    count = TILE // ROWS
    span = GROUP * ROWS
    rows = [block[ROWS * i : ROWS * i + ROWS, :] for i in range(count)]
    lane = lax.broadcasted_iota(jnp.int32, (ROWS, TILE), 1)
    sub = lax.broadcasted_iota(jnp.int32, (ROWS, TILE), 0)
    units = [jnp.where(sub == t, jnp.float32(1.0), jnp.float32(0.0)) for t in range(ROWS)]
    b = [lanes(rows[0], j) for j in range(ROWS)]
    for first in range(0, count, GROUP):
        now = list(range(first, first + GROUP))
        soon = [i for i in range(first + GROUP, first + 2 * GROUP) if i < count]
        rest = [i for i in range(count) if i not in now and i not in soon]
        before = list(rows)
        for p in now:
            k = ROWS * p
            inside = (lane >= k) & (lane < k + ROWS)
            r = rows[p]
            ahead = []
            if p + 1 < count:
                ahead = [lanes(r, k + ROWS + j) for j in range(ROWS)]
                below = [lanes(rows[p + 1], k + j) for j in range(ROWS)]
                beyond = [lanes(rows[p + 1], k + ROWS + j) for j in range(ROWS)]
            r = jnp.where(inside, jnp.where(lane - k == sub, jnp.float32(1.0), jnp.float32(0.0)), r)
            for t in range(0, ROWS, 2):
                top = subs(b[t], t)
                side = subs(b[t + 1], t)
                low = subs(b[t + 1], t + 1)
                inverse = 1.0 / (top * low - side * side)
                f = (b[t] - units[t]) * (1.0 / top)
                w = ((b[t + 1] - f * side) - units[t + 1]) * top
                g = w * inverse

                def eliminate(x, hurry=False):
                    x = x - f * subs(x, t)
                    other = subs(x, t + 1)
                    return x - ((w * other) * inverse if hurry else g * other)

                for j in range(t + 2, ROWS):
                    b[j] = eliminate(b[j], j < t + 4)
                r = eliminate(r)
                ahead = [eliminate(x) for x in ahead]
            if ahead:
                b = [
                    beyond[j] - tree_sum(below[m] * subs(ahead[j], m) for m in range(ROWS))
                    for j in range(ROWS)
                ]
            q = [subs(r, j) for j in range(ROWS)]
            for i in [i for i in now + soon if i > p] + [i for i in now if i < p]:
                e = rows[i]
                spread = below if i == p + 1 else [lanes(e, k + j) for j in range(ROWS)]
                kept = jnp.where(inside, jnp.float32(0.0), e)
                rows[i] = kept - tree_sum(spread[j] * q[j] for j in range(ROWS))
            rows[p] = r
        start = first * ROWS
        solved = jnp.concatenate([rows[i] for i in now], 0)
        for part in ([i for i in rest if i > first], [i for i in rest if i < first]):
            if part:
                c = jnp.concatenate([before[i] for i in part], 0)
                wide = lax.broadcasted_iota(jnp.int32, c.shape, 1)
                done = (wide >= start) & (wide < start + span)
                update = short_matmul(c[:, start : start + span], solved)
                c = jnp.where(done, jnp.float32(0.0), c) - update
                for m, i in enumerate(part):
                    rows[i] = c[ROWS * m : ROWS * m + ROWS, :]
    return jnp.concatenate(rows, 0)


def sweep(a_ref, block, row_start):
    col_start = pl.multiple_of(block * TILE, TILE)
    row_start = pl.multiple_of(row_start, 64)
    rows = pl.ds(row_start, TILE)
    cols = pl.ds(col_start, TILE)
    inverse = invert_tile(a_ref[rows, cols])
    solved = thin_matmul(inverse, a_ref[rows, :])
    column = a_ref[:, cols]
    a_ref[:, cols] = jnp.zeros_like(column)
    lane = lax.broadcasted_iota(jnp.int32, solved.shape, 1)
    inside = (lane >= col_start) & (lane < col_start + TILE)
    tiled = jnp.concatenate([inverse] * (solved.shape[1] // TILE), axis=1)
    solved = jnp.where(inside, tiled, solved)
    a_ref[...] = a_ref[...] - thin_matmul(column, solved)
    a_ref[rows, :] = solved


SMEM = pl.BlockSpec(memory_space=pltpu.SMEM)
VMEM = pl.BlockSpec(memory_space=pltpu.VMEM)
HALF, CORE, LIVE, LIVE_FAR, LONE = range(5)


def local_call(body, name, micros, flags, inputs, shapes, scratch=()):
    out = pl.pallas_call(
        body,
        out_shape=[jax.ShapeDtypeStruct(shape, jnp.float32) for shape in shapes],
        in_specs=[SMEM] + [VMEM] * len(inputs),
        out_specs=[VMEM] * len(shapes),
        scratch_shapes=[pltpu.VMEM(shape, jnp.float32) for shape in scratch],
        compiler_params=pltpu.CompilerParams(vmem_limit_bytes=VMEM_BYTES),
        cost_estimate=pl.CostEstimate(
            flops=int(micros * 1.1e9), transcendentals=0, bytes_accessed=int(micros * 3.5e6)
        ),
        name=name,
    )(flags, *inputs)
    return out


def rows_of(half, size):
    return pl.ds(pl.multiple_of(half * size, 64), size)


def lone_diag(flags, offset, shape):
    row = lax.broadcasted_iota(jnp.int32, shape, 0) + offset
    col = lax.broadcasted_iota(jnp.int32, shape, 1)
    lone = jnp.where(flags[LONE] == 1, jnp.float32(1.0), jnp.float32(0.0))
    return jnp.where(row == col, lone, jnp.float32(0.0))


def factor_of(flag):
    return jnp.where(flag == 1, jnp.float32(1.0), jnp.float32(0.0))


def first_kernel(flags, own_ref, out_ref):
    half = flags[HALF]
    size = own_ref.shape[0]
    out_ref[...] = own_ref[...] + lone_diag(flags, half * size, own_ref.shape)

    def body(step, carry):
        block = jnp.where(half == 0, step, 4 - step)
        sweep(out_ref, block, block * TILE - half * size)
        return carry

    lax.fori_loop(0, 2, body, 0)


def complete(half, own_ref, square, turned_ref, full_ref):
    size = own_ref.shape[0]
    own = own_ref[...]
    turned_ref[...] = own.T
    full_ref[rows_of(half, size), :] = own

    @pl.when(half == 0)
    def _():
        full_ref[size:, :size] = turned_ref[size:, :]
        full_ref[size:, size:] = square

    @pl.when(half == 1)
    def _():
        full_ref[:size, size:] = turned_ref[:size, :]
        full_ref[:size, :size] = square


def second_kernel(first_col, flags, own_ref, swept_ref, square_ref, out_ref, turned_ref):
    half = flags[HALF]
    size = own_ref.shape[0]
    square = square_ref[:, first_col : first_col + size]
    complete(half, own_ref, square, turned_ref, out_ref)
    other_rows = rows_of(1 - half, size)
    done_cols = pl.multiple_of(half * 384, TILE)
    column = out_ref[other_rows, pl.ds(done_cols, 256)]
    solved = swept_ref[pl.ds(pl.multiple_of(half * 64, 64), 256), :]
    shape = own_ref.shape
    lane = lax.broadcasted_iota(jnp.int32, shape, 1)
    done = (lane >= done_cols) & (lane < done_cols + 256)
    other = out_ref[other_rows, :] + lone_diag(flags, (1 - half) * size, shape)
    out_ref[rows_of(half, size), :] = swept_ref[...]
    out_ref[other_rows, :] = jnp.where(done, jnp.float32(0.0), other) - six_pass(column, solved)

    def body(step, carry):
        block = jnp.where(half == 0, 2 + step, 2 - step)
        sweep(out_ref, block, block * TILE)
        return carry

    lax.fori_loop(0, 3, body, 0)


def rest_kernel(flags, inverse_ref, x_ref, square_ref, g_ref, rest_ref, turned_ref, full_ref):
    half = flags[HALF]
    size, width = x_ref.shape
    complete(half, x_ref, square_ref[...], turned_ref, full_ref)
    g_ref[...] = factor_of(flags[LIVE]) * six_pass(full_ref[...], inverse_ref[...])
    own_rows, other_rows = rows_of(half, size), rows_of(1 - half, size)
    rest_ref[:, :width] = x_ref[...] - six_pass(g_ref[own_rows, :], full_ref[...])
    rest_ref[:, width : width + size] = square_ref[...] - six_pass(
        g_ref[other_rows, :], full_ref[other_rows, :], across=True
    )
    rest_ref[:, width + size :] = jnp.zeros_like(rest_ref[:, width + size :])


def link_kernel(flags, g_ref, y_ref, y_square_ref, link_ref, turned_link_ref, turned_ref, full_ref):
    complete(flags[HALF], y_ref, y_square_ref[...], turned_ref, full_ref)
    live = -factor_of(flags[LIVE_FAR])
    g = g_ref[...]
    link_ref[...] = live * three_pass(g, full_ref[...])
    turned_link_ref[...] = live * three_pass(y_ref[...], g, across=True)


def combine_kernel(flags, rest_ref, came_ref, diag_ref, link_ref, own_out, packed_out):
    size, width = own_out.shape
    row = lax.broadcasted_iota(jnp.int32, (size, width), 0) + flags[HALF] * size
    col = lax.broadcasted_iota(jnp.int32, (size, width), 1)
    own_diag = jnp.where(row == col, diag_ref[:, :width], jnp.float32(0.0))
    own_out[...] = rest_ref[:, :width] + came_ref[:, :width] + own_diag
    tail = rest_ref.shape[1] - width
    row = lax.broadcasted_iota(jnp.int32, (size, tail), 0)
    col = lax.broadcasted_iota(jnp.int32, (size, tail), 1)
    square_diag = jnp.where(row == col, diag_ref[:, width:], jnp.float32(0.0))
    packed_out[:, :width] = link_ref[...]
    packed_out[:, width:] = rest_ref[:, width:] + came_ref[:, width:] + square_diag


def near_kernel(flags, g_ref, loads_ref, part_ref):
    part_ref[...] = three_pass(g_ref[...], loads_ref[...])


def post_kernel(flags, inverse_ref, link_ref, far_ref, diag_ref, g_ref, kept_ref, sent_ref, part_ref):
    half, core = flags[HALF], flags[CORE]
    size, width = diag_ref.shape
    link = link_ref[...]
    both = parted_three_pass(jnp.concatenate([link, far_ref[:, :width]], 0), inverse_ref[...])
    g_ref[...] = both[:width]
    left = jnp.concatenate([g_ref[rows_of(half, size), :], both[width:]], 0)
    part_ref[...] = parted_three_pass(left, link, across=True)
    part = size // 2
    keep = pl.multiple_of(core * part, 32)
    send = pl.multiple_of((1 - core) * part, 32)
    kept_ref[:part, :] = diag_ref[pl.ds(keep, part), :] - part_ref[pl.ds(keep, part), :]
    kept_ref[part:, :] = -part_ref[pl.ds(size + keep, part), :]
    sent_ref[:part, :] = -part_ref[pl.ds(send, part), :]
    sent_ref[part:, :] = -part_ref[pl.ds(size + send, part), :]


def last_kernel(flags, g_ref, loads_ref, near_ref, kept_ref, sent_ref, part_ref):
    core = flags[CORE]
    width = kept_ref.shape[1]
    part_ref[...] = three_pass(g_ref[...], near_ref[...])
    keep = pl.ds(pl.multiple_of(core * width, width), width)
    send = pl.ds(pl.multiple_of((1 - core) * width, width), width)
    kept_ref[...] = loads_ref[:, keep] - part_ref[:, keep]
    sent_ref[...] = -part_ref[:, send]


def device(layer, half, core):
    return layer * 4 + half * 2 + core


def pairs_of(count, moves):
    pairs = []
    for layer in range(count):
        for half in range(2):
            for core, up, across, onto in moves:
                if 0 <= layer + up < count:
                    pairs.append(
                        (device(layer, half, core), device(layer + up, half ^ across, onto))
                    )
    return pairs


def after(array, *others):
    return lax.optimization_barrier((array,) + others)[0]


def shards(coupling, density, support, loads):
    part = coupling.shape[1]
    width = coupling.shape[2]
    layers = lax.axis_size("layer")
    layer = lax.axis_index("layer")
    place = lax.axis_index("rhs")
    half = place // 2
    core = place % 2
    upper = core == 1

    def move(array, *moves):
        return lax.ppermute(array, AXES, pairs_of(layers, moves))

    def straight(array, by):
        return move(array, (0, by, 0, 0), (1, -by, 0, 1))

    def crossed(array, by):
        return move(array, (1, by, 0, 0), (0, -by, 0, 1))

    def sibling(array):
        return move(array, (0, 0, 0, 1), (1, 0, 0, 0))

    def opposite(array):
        return move(array, (0, 0, 1, 0), (1, 0, 1, 1))

    def flipped(array):
        pairs = pairs_of(layers, [(1, 1, 1, 0), (0, -1, 1, 1)])
        for side in range(2):
            pairs.append((device(layers - 1, side, 1), device(layers - 1, 1 - side, 1)))
        return lax.ppermute(array, AXES, pairs)

    def pick(on_upper, on_lower):
        return jnp.where(upper, on_upper, on_lower)

    span = 2 * part
    cases = loads.shape[2]

    def square(array, first):
        return jnp.where(first == 0, array[:, :span], array[:, span:])

    live = jnp.logical_not(upper & (layer == layers - 1))
    live_far = jnp.logical_not(upper & (layer == layers - 2))
    lone = jnp.logical_not(pick(layer + 2 < layers, layer >= 2))
    zero = jnp.zeros((), jnp.int32)
    flags_0 = jnp.stack([half, core, live, live_far, zero]).astype(jnp.int32)
    flags_1 = jnp.stack([half, core, live, live_far, lone]).astype(jnp.int32)
    row = lax.broadcasted_iota(jnp.int32, (span, width), 0)
    col = lax.broadcasted_iota(jnp.int32, (span, width), 1)
    own_diag = col == row + half * span
    square_diag = row[:, :span] == col[:, :span]

    rho = 0.3 + 0.7 * density[0].astype(jnp.float32)
    rho_rows = lax.dynamic_slice_in_dim(rho, place * part, part, 0)
    stiff = rho_rows[:, None] * coupling[0] * rho[None, :]
    ones = jnp.ones((ROWS - 1, width), jnp.float32)
    tagged = jnp.concatenate([stiff, support, ones], axis=0)

    near_a = straight(tagged, 1)
    near_b = crossed(stiff, 1)
    far_a = move(stiff, (0, 2, 0, 0))
    far_b = move(stiff, (1, 2, 0, 0), (0, 0, 0, 1))
    side_support = jnp.where(near_a[part + 1] > 0.5, near_a[part], jnp.float32(1.0))
    near_a = near_a[:part]
    x_own = jnp.concatenate([pick(far_b, near_a), pick(stiff, near_b)], axis=0)
    y_own = jnp.concatenate([pick(near_b, far_a), pick(near_a, far_b)], axis=0)
    d_own = (x_own + y_own) + jnp.where(own_diag, side_support[None, :], jnp.float32(0.0))

    d_square = opposite(square(d_own, half))
    own_shape = (span, width)
    full_shape = (width, width)
    packed_shape = (span, width + 3 * TILE)
    load_shape = (width, cases)
    pair_shape = (width, 2 * cases)
    turned_shape = (width, span)

    loads_0 = loads[0]
    loads_in = sibling(loads_0)
    loads_0 = jnp.concatenate([pick(loads_in, loads_0), pick(loads_0, loads_in)], axis=1)
    (swept_0,) = local_call(first_kernel, "invert_first", 9, flags_0, [d_own], [own_shape])
    x_square = flipped(after(square(x_own, half), swept_0))
    near_loads = straight(after(loads_0, swept_0), 1)
    (inverse,) = local_call(
        functools.partial(second_kernel, 0), "invert_second", 14, flags_0,
        [d_own, swept_0, d_square], [full_shape], [turned_shape],
    )
    g_full, rest = local_call(
        rest_kernel, "rest", 1, flags_0, [inverse, x_own, x_square],
        [full_shape, packed_shape], [turned_shape, full_shape],
    )
    rest_in = sibling(rest)
    other_side = jnp.where(half == 0, side_support[span:], side_support[:span])
    y_square = (d_square - x_square) - jnp.where(square_diag, other_side[None, :], jnp.float32(0.0))
    link, turned_link = local_call(
        link_kernel, "links", 5, flags_0, [g_full, after(y_own, near_loads), y_square],
        [full_shape, own_shape], [turned_shape, full_shape],
    )
    other_support = jnp.where(half == 0, support[:, span:], support[:, :span])
    rest_diag = jnp.concatenate([support, other_support, jnp.zeros((1, 3 * TILE - span))], axis=1)
    new_own, packed = local_call(
        combine_kernel, "combine", 1, flags_0, [rest, rest_in, rest_diag, turned_link],
        [own_shape, packed_shape],
    )
    d_own = straight(new_own, 2)
    packed = straight(packed, 2)
    (near_part,) = local_call(
        near_kernel, "near_loads", 2, flags_0, [after(g_full, new_own), near_loads], [pair_shape]
    )
    new_loads = loads_0 + near_part + sibling(near_part)

    (swept,) = local_call(first_kernel, "invert_first", 9, flags_1, [d_own], [own_shape])
    near_loads = straight(after(new_loads, swept), 2)
    (inverse,) = local_call(
        functools.partial(second_kernel, width), "invert_second", 14, flags_1,
        [d_own, swept, packed], [full_shape], [turned_shape],
    )
    g_full, kept, sent = local_call(
        post_kernel, "last_blocks", 6, flags_1, [inverse, link, packed, new_own],
        [full_shape, own_shape, own_shape], [full_shape],
    )
    came = sibling(sent)
    load_kept, load_sent = local_call(
        last_kernel, "last_loads", 2, flags_1, [g_full, new_loads, near_loads],
        [load_shape, load_shape], [pair_shape],
    )
    loads_out = load_kept + sibling(load_sent)
    diag_out = kept[:part] + came[:part]
    lower_out = pick(came[part:], kept[part:])
    upper_out = pick(kept[part:], came[part:])
    return (diag_out[None], lower_out[None], upper_out[None], loads_out[None])


def solution(mesh):
    placed = (P("layer", "rhs", None), P("layer", None), P("layer", None), P("layer", None, "rhs"))
    return jax.shard_map(
        shards,
        mesh=mesh,
        in_specs=placed,
        out_specs=(
            P("layer", "rhs", None),
            P("layer", "rhs", None),
            P("layer", "rhs", None),
            P("layer", None, "rhs"),
        ),
        check_vma=False,
    )
```
